128 devices in a mesh: section: 4 (over y_lo, core), seq: 32 (over x, y_hi, z).
Axes of the slice: x: 4, y: 4 (y_hi: 2, y_lo: 2; y = y_hi * 2 + y_lo), z: 4, core: 2. Of those that a mesh axis runs over, the one named last changes fastest.
Arguments:
- acts: bfloat16 [4, 4096, 4096], P('section', 'seq'), may hold values from -40 to 40
- gains: float32 [4, 4096], P('section'), may hold values from 0.5 to 1.5
- grad_top: bfloat16 [4096, 4096], P('seq'), may hold values from -6 to 6
- keys: bfloat16 [3072, 4096], P('seq'), may hold values from -40 to 40
- values: bfloat16 [3072, 4096], P('seq'), may hold values from -6 to 6
- offsets: int32 [32], replicated, may hold values from 0 to 2944
Outputs:
- grad_acts: bfloat16 [4, 4096, 4096], P('section', 'seq')
- grad_keys: bfloat16 [3072, 4096], P('seq')
- grad_values: bfloat16 [3072, 4096], P('seq')
The draws below stay inside these ranges and needn't reach their ends.
All inputs are finite; a program needn't handle non-finite values.
Results may differ from the reference program's by a relative error of at most 0.015.
Values may be sent and summed in bfloat16 or wider, within the bound.
A program may use at most 128 MiB of HBM per device.

```python
import jax
import jax.numpy as jnp
from jax import lax

H = 32
DH = 128
TQ_DEV = 128
F = 4096
SECTIONS = 4
QLEN = 4096
KLEN = 3072


def draw_acts(key, part):
    key = jax.random.fold_in(key, 1)
    first = jax.random.fold_in(key, 0)
    base = jnp.clip(jax.random.normal(first, (SECTIONS, QLEN, F), jnp.float32), -4.0, 4.0)
    return base.astype(jnp.bfloat16)


def draw_keys(key, part):
    key = jax.random.fold_in(key, 2)
    first = jax.random.fold_in(key, 0)
    base = jnp.clip(jax.random.normal(first, (KLEN, F), jnp.float32), -4.0, 4.0)
    return base.astype(jnp.bfloat16)


def touch_ends(drawn, key, smallest, largest):
    longest = drawn.shape.index(max(drawn.shape))
    spots = []
    for shift in (0, 1):
        where = [jax.random.randint(jax.random.fold_in(key, axis), (), 0, length) for axis, length in enumerate(drawn.shape)]
        where[longest] = (where[longest] + shift) % drawn.shape[longest]
        spots.append(tuple(where))
    return drawn.at[spots[0]].set(smallest).at[spots[1]].set(largest)


def levels(stream_key, extent, shards, smallest, top_value):
    def one(dim, parts):
        draws = jax.random.uniform(jax.random.fold_in(jax.random.fold_in(stream_key, 6), dim), (parts,), jnp.float32, smallest / len(shards), top_value / len(shards))
        return jnp.repeat(jnp.exp(draws), extent[dim] // parts).reshape((-1,) + (1,) * (len(extent) - dim - 1))

    factor_of = one(*shards[0])
    for cut in shards[1:]:
        factor_of = factor_of * one(*cut)
    return factor_of


def scatter_about(own_key, extent, deviation, most, shards=(), kind=jnp.bfloat16):
    loudness = levels(own_key, extent, shards, -0.22, 0.18) if shards else 1.0
    values = jax.random.normal(own_key, extent, jnp.float32) * deviation * loudness
    return jnp.minimum(jnp.maximum(values, -most), most).astype(kind)


def setup_inputs(seed: int = 0) -> dict:
    key_list = jax.random.split(jax.random.key(seed), 7)
    acts = draw_acts(jax.random.fold_in(key_list[6], 71), 0)
    gains = jnp.clip(1.0 + 0.1 * jax.random.normal(key_list[1], (SECTIONS, F), jnp.float32), 0.5, 1.5)
    grad_top = scatter_about(key_list[2], (QLEN, F), 1.0, 6.0, ((0, 32),))
    keys = draw_keys(jax.random.fold_in(key_list[6], 71), 0)
    values = scatter_about(key_list[4], (KLEN, F), 1.0, 6.0, ((0, 32),))
    offsets = touch_ends(jax.random.randint(key_list[5], (QLEN // TQ_DEV,), 0, KLEN - TQ_DEV + 1), jax.random.fold_in(key_list[5], 1), 0, KLEN - TQ_DEV).astype(jnp.int32)
    return dict(acts=acts, gains=gains, grad_top=grad_top, keys=keys, values=values, offsets=offsets)


def head_grads(operands):
    qh, douth, kh, vh, allowed = operands
    scale = 1.0 / (DH ** 0.5)
    scores = jnp.dot(qh, kh.T, preferred_element_type=jnp.float32) * scale
    scores = jnp.where(allowed, scores, -1e30)
    peak = jnp.max(scores, axis=1, keepdims=True)
    weights = jnp.where(allowed, jnp.exp(scores - peak), 0.0)
    probs = weights / jnp.sum(weights, axis=1, keepdims=True)
    probs_round = probs.astype(jnp.bfloat16)
    dprobs = jnp.dot(douth, vh.T, preferred_element_type=jnp.float32)
    delta = jnp.sum(probs * dprobs, axis=1, keepdims=True)
    dscore = (probs * (dprobs - delta) * scale).astype(jnp.bfloat16)
    dquery = jnp.dot(dscore, kh, preferred_element_type=jnp.float32)
    dkey = jnp.dot(dscore.T, qh, preferred_element_type=jnp.float32)
    dvalue = jnp.dot(probs_round.T, douth, preferred_element_type=jnp.float32)
    return dquery, dkey, dvalue


def reference(acts, gains, grad_top, keys, values, offsets):
    qpos = (offsets[:, None] + jnp.arange(TQ_DEV, dtype=jnp.int32)[None, :]).reshape(-1)
    allowed = jnp.arange(KLEN, dtype=jnp.int32)[None, :] <= qpos[:, None]
    key_heads = keys.reshape(KLEN, H, DH).transpose(1, 0, 2)
    value_heads = values.reshape(KLEN, H, DH).transpose(1, 0, 2)
    upstream = grad_top
    total_keys = jnp.zeros((KLEN, F), jnp.float32)
    total_values = jnp.zeros((KLEN, F), jnp.float32)
    results = []
    for layer_num in reversed(range(SECTIONS)):
        query = (acts[layer_num].astype(jnp.float32) * gains[layer_num][None, :]).astype(jnp.bfloat16)
        query_heads = query.reshape(QLEN, H, DH).transpose(1, 0, 2)
        up_heads = upstream.reshape(QLEN, H, DH).transpose(1, 0, 2)

        def one_head(items):
            return head_grads((items[0], items[1], items[2], items[3], allowed))

        dquery, dkey, dvalue = lax.map(one_head, (query_heads, up_heads, key_heads, value_heads))
        dquery = dquery.transpose(1, 0, 2).reshape(QLEN, F)
        total_keys = total_keys + dkey.transpose(1, 0, 2).reshape(KLEN, F)
        total_values = total_values + dvalue.transpose(1, 0, 2).reshape(KLEN, F)
        upstream = (upstream.astype(jnp.float32) + gains[layer_num][None, :] * dquery).astype(jnp.bfloat16)
        results.append(upstream)
    grad_acts = jnp.stack(results[::-1], axis=0)
    return grad_acts, total_keys.astype(jnp.bfloat16), total_values.astype(jnp.bfloat16)
```

```python
import jax
import jax.numpy as jnp
from jax import lax
from jax.experimental import pallas as pl
from jax.experimental.pallas import tpu as pltpu
from jax.sharding import PartitionSpec as P

DH = 128
SECT = 4
NB = 32
RB = 32
KLEN = 3072
TILE = 256
GRP = TILE // RB
CH = 1024
SCALE = 1.0 / DH**0.5
LOG2E = 1.4426950408889634
NT = (((1,), (1,)), ((), ()))
NN = (((1,), (0,)), ((), ()))


def fdot(a, b, dims=NN):
    return lax.dot_general(a, b, dims, preferred_element_type=jnp.float32)


def fold(x, op):
    return op(x.reshape(x.shape[0] // 8, 8, x.shape[1]), axis=0)


def compute_kernel(order, offs, q_in, top, keys, vals, gains, grad, dkv_out,
                   kt, sc, ex, dp, dk, dv, q_s, up_s, qn_s, un_s, dqt):
    first = lax.axis_index("section") * RB
    kt[...] = keys[...].T
    dk[...] = jnp.zeros_like(dk)
    dv[...] = jnp.zeros_like(dv)
    lane = lax.broadcasted_iota(jnp.int32, (1, TILE), 1)

    def tile_step(t, _):
        qpos = lax.rem(lane, RB) + first
        group = lax.div(lane, RB)
        for k in range(GRP):
            block = order[t * GRP + k]
            qpos = qpos + jnp.where(group == k, offs[block], 0)
            up_s[k * RB : (k + 1) * RB, :] = top[block]
        low = offs[order[t * GRP]] + first
        high = offs[order[t * GRP + GRP - 1]] + first + RB
        full = lax.div(low + 1, CH)
        total = lax.div(high + CH - 1, CH)

        def layer_step(turn, _):
            layer = SECT - 1 - turn
            gain = gains[layer][0:1, :]
            for k in range(GRP):
                block = order[t * GRP + k]
                q_s[k * RB : (k + 1) * RB, :] = (
                    q_in[layer, block].astype(jnp.float32) * gain
                ).astype(jnp.bfloat16)

            def scores(j, peak, masked):
                rows = pl.ds(pl.multiple_of(j * CH, CH), CH)
                s = fdot(keys[rows, :], q_s[...], NT)
                if masked:
                    spot = lax.broadcasted_iota(jnp.int32, (CH, TILE), 0) + j * CH
                    s = jnp.where(spot <= qpos, s, -1e30)
                sc[rows, :] = s
                return jnp.maximum(peak, fold(s, jnp.max))

            peak = jnp.full((8, TILE), -1e30, jnp.float32)
            peak = lax.fori_loop(0, full, lambda j, c: scores(j, c, False), peak)
            peak = lax.fori_loop(full, total, lambda j, c: scores(j, c, True), peak)
            peak = jnp.max(peak, axis=0, keepdims=True)

            def weights(j, carry):
                rows = pl.ds(pl.multiple_of(j * CH, CH), CH)
                e = jnp.exp2((sc[rows, :] - peak) * (SCALE * LOG2E))
                d = fdot(vals[rows, :], up_s[...], NT)
                ex[rows, :] = e.astype(jnp.bfloat16)
                dp[rows, :] = d
                return carry[0] + fold(e, jnp.sum), carry[1] + fold(e * d, jnp.sum)

            zero = jnp.zeros((8, TILE), jnp.float32)
            norm, delta = lax.fori_loop(0, total, weights, (zero, zero))
            inv = 1.0 / jnp.sum(norm, axis=0, keepdims=True)
            delta = jnp.sum(delta, axis=0, keepdims=True) * inv
            inv_rows = jnp.broadcast_to(inv, (DH, TILE)).T
            qn_s[...] = (q_s[...].astype(jnp.float32) * (inv_rows * SCALE)).astype(jnp.bfloat16)
            un_s[...] = (up_s[...].astype(jnp.float32) * inv_rows).astype(jnp.bfloat16)
            dqt[...] = jnp.zeros_like(dqt)

            def grads(j, _):
                rows = pl.ds(pl.multiple_of(j * CH, CH), CH)
                e = ex[rows, :]
                ds = (e.astype(jnp.float32) * (dp[rows, :] - delta)).astype(jnp.bfloat16)
                dqt[...] += fdot(kt[:, rows], ds)
                dk[rows, :] += fdot(ds, qn_s[...])
                dv[rows, :] += fdot(e, un_s[...])
                return 0

            lax.fori_loop(0, total, grads, 0)
            dq = (dqt[...] * (inv * SCALE)).T
            up = (up_s[...].astype(jnp.float32) + gain * dq).astype(jnp.bfloat16)
            up_s[...] = up
            for k in range(GRP):
                grad[layer, order[t * GRP + k]] = up[k * RB : (k + 1) * RB, :]
            return 0

        lax.fori_loop(0, SECT, layer_step, 0)
        return 0

    lax.fori_loop(0, NB * RB // TILE, tile_step, 0)
    dkv_out[0] = dk[...].astype(jnp.bfloat16)
    dkv_out[1] = dv[...].astype(jnp.bfloat16)


def compute(order, offs, q_in, top, keys, vals, gains):
    smem = pl.BlockSpec(memory_space=pltpu.SMEM)
    vmem = pl.BlockSpec(memory_space=pltpu.VMEM)
    return pl.pallas_call(
        compute_kernel,
        out_shape=(
            jax.ShapeDtypeStruct((SECT, NB, RB, DH), jnp.bfloat16),
            jax.ShapeDtypeStruct((2, KLEN, DH), jnp.bfloat16),
        ),
        in_specs=[smem, smem] + [vmem] * 5,
        out_specs=(vmem, vmem),
        scratch_shapes=[
            pltpu.VMEM((DH, KLEN), jnp.bfloat16),
            pltpu.VMEM((KLEN, TILE), jnp.float32),
            pltpu.VMEM((KLEN, TILE), jnp.bfloat16),
            pltpu.VMEM((KLEN, TILE), jnp.float32),
            pltpu.VMEM((KLEN, DH), jnp.float32),
            pltpu.VMEM((KLEN, DH), jnp.float32),
            pltpu.VMEM((TILE, DH), jnp.bfloat16),
            pltpu.VMEM((TILE, DH), jnp.bfloat16),
            pltpu.VMEM((TILE, DH), jnp.bfloat16),
            pltpu.VMEM((TILE, DH), jnp.bfloat16),
            pltpu.VMEM((DH, TILE), jnp.float32),
        ],
        compiler_params=pltpu.CompilerParams(vmem_limit_bytes=56 * 2**20),
    )(order, offs, q_in, top, keys, vals, gains)


SEQ = 32
HALF = 48
ALL = SECT * SEQ
MESH = pl.DeviceIdType.MESH


def greet(section, seq):
    barrier = pltpu.get_barrier_semaphore()
    me = section * SEQ + seq

    def hello(i, _):
        peer = lax.rem(me + i, ALL)
        pl.semaphore_signal(
            barrier, inc=1, device_id=(lax.div(peer, SEQ), lax.rem(peer, SEQ)), device_id_type=MESH
        )
        return 0

    lax.fori_loop(1, ALL, hello, 0)
    pl.semaphore_wait(barrier, ALL - 1)


def push(src, dst, send, recv, device):
    pltpu.make_async_remote_copy(
        src_ref=src, dst_ref=dst, send_sem=send, recv_sem=recv, device_id=device, device_id_type=MESH
    ).start()


def arrived(ref, sem):
    pltpu.make_async_copy(ref, ref, sem).wait()


def columns(head):
    return pl.ds(pl.multiple_of(head * DH, DH), DH)


def spread_kernel(acts, top, keys, vals, gain, q_out, top_out, k_out, v_out, g_out, send, recv):
    section, seq = lax.axis_index("section"), lax.axis_index("seq")
    core = lax.rem(section, 2)
    sibling = section + 1 - 2 * core
    greet(section, seq)

    def cached(i, _):
        head = lax.rem(seq + i, SEQ)
        push(keys.at[core, :, columns(head)], k_out.at[seq, core], send.at[0], recv.at[0], (section, head))
        push(vals.at[core, :, columns(head)], v_out.at[seq, core], send.at[1], recv.at[1], (section, head))
        return 0

    def queries(i, _):
        head = lax.rem(seq + i, SEQ)
        push(
            top.at[pl.ds(pl.multiple_of(section * RB, RB), RB), columns(head)],
            top_out.at[seq], send.at[2], recv.at[2], (section, head),
        )
        for j in range(SECT):
            group = lax.rem(section + j, SECT)
            push(
                acts.at[pl.ds(pl.multiple_of(group * RB, RB), RB), columns(head)],
                q_out.at[section * SEQ + seq], send.at[3], recv.at[3], (group, head),
            )
        return 0

    mine = pl.ds(pl.multiple_of(section * RB, RB), RB)
    pltpu.make_async_copy(keys.at[core, :, columns(seq)], k_out.at[seq, core], recv.at[0]).start()
    pltpu.make_async_copy(vals.at[core, :, columns(seq)], v_out.at[seq, core], recv.at[1]).start()
    pltpu.make_async_copy(top.at[mine, columns(seq)], top_out.at[seq], recv.at[2]).start()
    pltpu.make_async_copy(acts.at[mine, columns(seq)], q_out.at[section * SEQ + seq], recv.at[3]).start()
    pltpu.make_async_copy(gain, g_out.at[section], recv.at[4]).start()
    lax.fori_loop(1, SEQ, cached, 0)
    for j in range(1, SECT):
        group = lax.rem(section + j, SECT)
        push(gain, g_out.at[section], send.at[4], recv.at[4], (group, seq))
        push(
            acts.at[pl.ds(pl.multiple_of(group * RB, RB), RB), columns(seq)],
            q_out.at[section * SEQ + seq], send.at[3], recv.at[3], (group, seq),
        )
    lax.fori_loop(1, SEQ, queries, 0)
    arrived(k_out.at[:, core], recv.at[0])
    push(k_out.at[:, core], k_out.at[:, core], send.at[5], recv.at[5], (sibling, seq))
    arrived(v_out.at[:, core], recv.at[1])
    push(v_out.at[:, core], v_out.at[:, core], send.at[6], recv.at[6], (sibling, seq))
    arrived(top_out, recv.at[2])
    arrived(q_out, recv.at[3])
    arrived(g_out, recv.at[4])
    arrived(k_out.at[:, 1 - core], recv.at[5])
    arrived(v_out.at[:, 1 - core], recv.at[6])
    arrived(k_out.at[: SEQ - 1, core], send.at[0])
    arrived(v_out.at[: SEQ - 1, core], send.at[1])
    arrived(top_out.at[: SEQ - 1], send.at[2])
    arrived(q_out.at[: ALL - 1], send.at[3])
    arrived(g_out.at[: SECT - 1], send.at[4])
    arrived(k_out.at[:, core], send.at[5])
    arrived(v_out.at[:, core], send.at[6])


def spread(acts, top, keys, vals, gain):
    any_space = pl.BlockSpec(memory_space=pl.ANY)
    return pl.pallas_call(
        spread_kernel,
        out_shape=(
            jax.ShapeDtypeStruct((ALL, RB, DH), jnp.bfloat16),
            jax.ShapeDtypeStruct((SEQ, RB, DH), jnp.bfloat16),
            jax.ShapeDtypeStruct((SEQ, 2, HALF, DH), jnp.bfloat16),
            jax.ShapeDtypeStruct((SEQ, 2, HALF, DH), jnp.bfloat16),
            jax.ShapeDtypeStruct((SECT, 8, DH), jnp.float32),
        ),
        in_specs=[any_space] * 5,
        out_specs=(any_space,) * 5,
        scratch_shapes=[pltpu.SemaphoreType.DMA((7,)), pltpu.SemaphoreType.DMA((7,))],
        compiler_params=pltpu.CompilerParams(
            collective_id=0, has_side_effects=True, vmem_limit_bytes=56 * 2**20
        ),
    )(acts, top, keys, vals, gain)


def collect_kernel(grad, dkv, acts_out, kv_out, from_core, part, from_chip, total, send, recv):
    section, seq = lax.axis_index("section"), lax.axis_index("seq")
    core, chip = lax.rem(section, 2), lax.div(section, 2)
    sibling = section + 1 - 2 * core
    across = section + 2 - 4 * chip
    greet(section, seq)
    push(dkv.at[:, :, 1 - core], from_core, send.at[0], recv.at[0], (sibling, seq))
    mine = pl.ds(pl.multiple_of(section * RB, RB), RB)
    pltpu.make_async_copy(grad.at[section * SEQ + seq], acts_out.at[mine, columns(seq)], recv.at[1]).start()

    def rows_back(block, layer):
        push(
            grad.at[layer * SEQ + block], acts_out.at[mine, columns(seq)],
            send.at[1], recv.at[1], (layer, block),
        )

    def send_grads(i, _):
        block = lax.rem(seq + i, SEQ)
        for j in range(SECT):
            rows_back(block, lax.rem(section + j, SECT))
        return 0

    for j in range(1, SECT):
        rows_back(seq, lax.rem(section + j, SECT))
    lax.fori_loop(1, SEQ, send_grads, 0)

    arrived(from_core, recv.at[0])

    def add_core(i, _):
        for kv in range(2):
            part[kv, i] = (
                dkv[kv, i, core].astype(jnp.float32) + from_core[kv, i].astype(jnp.float32)
            ).astype(jnp.bfloat16)
        return 0

    lax.fori_loop(0, SEQ, add_core, 0)
    push(part.at[1 - chip], from_chip, send.at[2], recv.at[2], (across, seq))
    arrived(from_chip, recv.at[2])

    def add_chip(i, _):
        total[i] = (part[chip, i].astype(jnp.float32) + from_chip[i].astype(jnp.float32)).astype(jnp.bfloat16)
        return 0

    lax.fori_loop(0, SEQ, add_chip, 0)
    target = kv_out.at[chip, core, :, columns(seq)]
    pltpu.make_async_copy(total.at[seq], target, recv.at[3]).start()
    push(total.at[seq], target, send.at[3], recv.at[3], (across, seq))

    def send_totals(i, _):
        block = lax.rem(seq + i, SEQ)
        push(total.at[block], target, send.at[3], recv.at[3], (section, block))
        push(total.at[block], target, send.at[3], recv.at[3], (across, block))
        return 0

    lax.fori_loop(1, SEQ, send_totals, 0)
    arrived(kv_out.at[:, core], recv.at[3])
    push(kv_out.at[:, core], kv_out.at[:, core], send.at[4], recv.at[4], (sibling, seq))
    arrived(acts_out, recv.at[1])
    arrived(kv_out.at[:, 1 - core], recv.at[4])
    arrived(from_core, send.at[0])
    arrived(grad.at[: ALL - 1], send.at[1])
    arrived(from_chip, send.at[2])
    arrived(total, send.at[3])
    arrived(total.at[: SEQ - 1], send.at[3])
    arrived(kv_out.at[:, core], send.at[4])


def collect(grad, dkv):
    any_space = pl.BlockSpec(memory_space=pl.ANY)
    vmem = pl.BlockSpec(memory_space=pltpu.VMEM)
    return pl.pallas_call(
        collect_kernel,
        out_shape=(
            jax.ShapeDtypeStruct((SECT * RB, SEQ * DH), jnp.bfloat16),
            jax.ShapeDtypeStruct((2, 2, HALF, SEQ * DH), jnp.bfloat16),
        ),
        in_specs=[any_space, vmem],
        out_specs=(any_space, any_space),
        scratch_shapes=[
            pltpu.VMEM((2, SEQ, HALF, DH), jnp.bfloat16),
            pltpu.VMEM((2, SEQ, HALF, DH), jnp.bfloat16),
            pltpu.VMEM((SEQ, HALF, DH), jnp.bfloat16),
            pltpu.VMEM((SEQ, HALF, DH), jnp.bfloat16),
            pltpu.SemaphoreType.DMA((5,)),
            pltpu.SemaphoreType.DMA((5,)),
        ],
        compiler_params=pltpu.CompilerParams(
            collective_id=1, has_side_effects=True, vmem_limit_bytes=56 * 2**20
        ),
    )(grad, dkv)


def local(acts, gains, grad_top, keys, values, offsets):
    seq = lax.axis_index("seq")
    gain = jnp.broadcast_to(lax.dynamic_slice(gains, (0, seq * DH), (1, DH)), (8, DH))
    spot = jnp.arange(SEQ, dtype=jnp.int32)
    ahead = (offsets[None, :] < offsets[:, None]) | (
        (offsets[None, :] == offsets[:, None]) & (spot[None, :] < spot[:, None])
    )
    rank = jnp.sum(ahead.astype(jnp.int32), axis=1)
    order = jnp.sum(jnp.where(rank[None, :] == spot[:, None], spot[None, :], 0), axis=1)
    q_in, top, k_in, v_in, gain_all = spread(
        acts[0], grad_top, keys.reshape(2, HALF, -1), values.reshape(2, HALF, -1), gain
    )
    grad, dkv = compute(
        order, offsets, q_in.reshape(SECT, NB, RB, DH), top,
        k_in.reshape(KLEN, DH), v_in.reshape(KLEN, DH), gain_all,
    )
    out_acts, out_kv = collect(grad.reshape(ALL, RB, DH), dkv.reshape(2, SEQ, 2, HALF, DH))
    return (out_acts[None], out_kv[0].reshape(2 * HALF, -1), out_kv[1].reshape(2 * HALF, -1))


def solution(mesh):
    return jax.shard_map(
        local,
        mesh=mesh,
        in_specs=(
            P("section", "seq", None),
            P("section", None),
            P("seq", None),
            P("seq", None),
            P("seq", None),
            P(),
        ),
        out_specs=(P("section", "seq", None), P("seq", None), P("seq", None)),
        check_vma=False,
    )
```

```python
import jax
import jax.numpy as jnp
from jax import lax
from jax.experimental import pallas as pl
from jax.experimental.pallas import tpu as pltpu
from jax.sharding import PartitionSpec as P

DH = 128
SECT = 4
SEQ = 32
ALL = SECT * SEQ
RB = 32
HALF = 48
KHALF = SEQ * HALF
KLEN = 2 * KHALF
TILE = 256
GRP = TILE // RB
TILES = SEQ // GRP
STEPS = SECT * TILES
PIECES = 4
PBLOCKS = SEQ // PIECES
PROWS = PBLOCKS * HALF
SCALE = 1.0 / DH**0.5
LOG2E = 1.4426950408889634
NO_PEAK = -3e38
MESH = pl.DeviceIdType.MESH


def fdot(a, b):
    return lax.dot_general(a, b, (((1,), (0,)), ((), ())), preferred_element_type=jnp.float32)


def push(src, dst, send, recv, device):
    pltpu.make_async_remote_copy(
        src_ref=src, dst_ref=dst, send_sem=send, recv_sem=recv, device_id=device, device_id_type=MESH
    ).start()


def keep(src, dst, sem):
    pltpu.make_async_copy(src, dst, sem).start()


def arrived(ref, sem):
    pltpu.make_async_copy(ref, ref, sem).wait()


def columns(head):
    return pl.ds(pl.multiple_of(head * DH, DH), DH)


def rows_of(start, count):
    return pl.ds(pl.multiple_of(start, 16), count)


def fill_bias(offs, first, bias):
    sub = lax.broadcasted_iota(jnp.int32, (RB, 1), 0)
    wide = 512

    def tile_bias(t, _):
        def some(j, _):
            flat = lax.broadcasted_iota(jnp.int32, (1, wide), 1) + j * wide
            half = lax.div(flat, KHALF)
            inside = flat - half * KHALF
            spot = inside + lax.div(inside, HALF) * HALF + half * HALF
            cols = pl.ds(pl.multiple_of(j * wide, wide), wide)
            for k in range(GRP):
                qpos = sub + (first + offs[t * GRP + k])
                bias[t, k * RB : (k + 1) * RB, cols] = jnp.where(spot <= qpos, 0.0, -1e30)
            return 0

        lax.fori_loop(0, KLEN // wide, some, 0)
        return 0

    lax.fori_loop(0, TILES, tile_bias, 0)


def load_query(q_in, gains, step):
    layer, t = SECT - 1 - lax.div(step, TILES), lax.rem(step, TILES)
    q = q_in[pl.ds(layer * SEQ + t * GRP, GRP)].reshape(TILE, DH)
    return (q.astype(jnp.float32) * gains[layer][0:1, :]).astype(jnp.bfloat16)


def split_query(q):
    scaled = q.astype(jnp.float32) * (SCALE * LOG2E)
    high = scaled.astype(jnp.bfloat16)
    low = (scaled - high.astype(jnp.float32)).astype(jnp.bfloat16)
    return jnp.concatenate([high, low], axis=1)


def scores(t, slot, kk, q2_s, bias, sc):
    s = fdot(q2_s[...], kk[...]) + bias[t]
    sc[slot] = s
    peak = jnp.full((TILE, DH), NO_PEAK, jnp.float32)
    for c in range(KLEN // DH):
        peak = jnp.maximum(peak, s[:, c * DH : (c + 1) * DH])
    return peak


def one_step(step, peak, q_in, gains, k_in, grad, kk, vt, bias, sc, ex, dp, dkv, q2_s, up_s):
    layer, t = SECT - 1 - lax.div(step, TILES), lax.rem(step, TILES)
    after = jnp.minimum(step + 1, STEPS - 1)
    slot = lax.rem(step, 2)
    up_now = up_s[pl.ds(t * GRP, GRP)].reshape(TILE, DH)
    q2_s[...] = split_query(load_query(q_in, gains, after))
    norm = jnp.zeros((TILE, DH), jnp.float32)
    delta = jnp.zeros((TILE, DH), jnp.float32)
    d = fdot(up_now, vt[...])
    e = jnp.exp2(sc[slot] - peak)
    dp[...] = d
    ex[...] = e.astype(jnp.bfloat16)
    ed = e * d
    for c in range(KLEN // DH):
        norm = norm + e[:, c * DH : (c + 1) * DH]
        delta = delta + ed[:, c * DH : (c + 1) * DH]
    peak_after = scores(lax.rem(after, TILES), 1 - slot, kk, q2_s, bias, sc)
    inv = 1.0 / jnp.sum(norm, axis=1, keepdims=True)
    delta = jnp.sum(delta, axis=1, keepdims=True) * inv
    q = load_query(q_in, gains, step)
    qn = (q.astype(jnp.float32) * (inv * SCALE)).T.astype(jnp.bfloat16)
    un = (up_now.astype(jnp.float32) * inv).T.astype(jnp.bfloat16)
    e = ex[...]
    ds = e * (dp[...] - delta).astype(jnp.bfloat16)
    dq = fdot(ds, k_in[...])
    dkv[0] += fdot(qn, ds)
    dkv[1] += fdot(un, e)
    up = (up_now.astype(jnp.float32) + gains[layer][0:1, :] * (dq * (inv * SCALE))).astype(jnp.bfloat16)
    up = up.reshape(GRP, RB, DH)
    up_s[pl.ds(t * GRP, GRP)] = up
    grad[pl.ds(layer * SEQ + t * GRP, GRP)] = up
    return jnp.max(peak_after, axis=1, keepdims=True)


def fused_kernel(
    offs, acts, top, keys, vals, gain, acts_out, k_out, v_out,
    q_in, up_s, k_in, v_in, g_in, grad, kk, vt, bias, sc, ex, dp, dkv, q2_s,
    outgoing, from_core, part, from_chip, total, send, recv, ready,
):
    section, seq = lax.axis_index("section"), lax.axis_index("seq")
    core, chip = lax.rem(section, 2), lax.div(section, 2)
    sibling = section + 1 - 2 * core
    across = section + 2 - 4 * chip
    me = section * SEQ + seq
    mine = rows_of(section * RB, RB)

    barrier = pltpu.get_barrier_semaphore()

    def hello(i, _):
        pl.semaphore_signal(barrier, inc=1, device_id=(section, lax.rem(seq + i, SEQ)), device_id_type=MESH)
        return 0

    lax.fori_loop(1, SEQ, hello, 0)
    for j in range(1, SECT):
        pl.semaphore_signal(barrier, inc=1, device_id=(lax.rem(section + j, SECT), seq), device_id_type=MESH)
    fill_bias(offs, section * RB, bias)
    dkv[...] = jnp.zeros_like(dkv)
    pl.semaphore_wait(barrier, SEQ + SECT - 2)
    for j in range(1, SECT):
        pl.semaphore_signal(ready, inc=1, device_id=(lax.rem(section + j, SECT), seq), device_id_type=MESH)

    k_here = k_in.at[rows_of(core * KHALF + seq * HALF, HALF)]
    v_here = v_in.at[rows_of(core * KHALF + seq * HALF, HALF)]

    def send_cached(i, _):
        head = lax.rem(seq + i, SEQ)
        push(keys.at[core, :, columns(head)], k_here, send.at[0], recv.at[0], (section, head))
        push(vals.at[core, :, columns(head)], v_here, send.at[1], recv.at[1], (section, head))
        return 0

    def send_query(group, head):
        push(
            acts.at[rows_of(group * RB, RB), columns(head)], q_in.at[me],
            send.at[3], recv.at[3 + section], (group, head),
        )

    def send_queries():
        for j in range(1, SECT):
            send_query(lax.rem(section + j, SECT), seq)

        def some(i, _):
            for j in range(SECT):
                send_query(lax.rem(section + j, SECT), lax.rem(seq + i, SEQ))
            return 0

        lax.fori_loop(1, SEQ, some, 0)

    def send_top(i, _):
        head = lax.rem(seq + i, SEQ)
        push(top.at[mine, columns(head)], up_s.at[seq], send.at[2], recv.at[2], (section, head))
        return 0

    keep(keys.at[core, :, columns(seq)], k_here, recv.at[0])
    keep(vals.at[core, :, columns(seq)], v_here, recv.at[1])
    keep(top.at[mine, columns(seq)], up_s.at[seq], recv.at[2])
    keep(acts.at[mine, columns(seq)], q_in.at[me], recv.at[3 + section])
    keep(gain, g_in.at[section], recv.at[7])
    lax.fori_loop(1, SEQ, send_cached, 0)
    for j in range(1, SECT):
        push(gain, g_in.at[section], send.at[4], recv.at[7], (lax.rem(section + j, SECT), seq))
    pl.semaphore_wait(ready, SECT - 1)

    @pl.when(section == SECT - 1)
    def _():
        send_queries()

    lax.fori_loop(1, SEQ, send_top, 0)
    k_half, v_half = k_in.at[rows_of(core * KHALF, KHALF)], v_in.at[rows_of(core * KHALF, KHALF)]
    k_other, v_other = k_in.at[rows_of((1 - core) * KHALF, KHALF)], v_in.at[rows_of((1 - core) * KHALF, KHALF)]
    arrived(k_half, recv.at[0])
    push(k_half, k_half, send.at[5], recv.at[8], (sibling, seq))
    arrived(v_half, recv.at[1])
    push(v_half, v_half, send.at[6], recv.at[9], (sibling, seq))

    @pl.when(section != SECT - 1)
    def _():
        send_queries()

    arrived(k_other, recv.at[8])
    kt = k_in[...].T
    kk[:DH, :] = kt
    kk[DH:, :] = kt
    arrived(v_other, recv.at[9])
    vt[...] = v_in[...].T
    arrived(g_in, recv.at[7])
    arrived(q_in.at[pl.ds((SECT - 1) * SEQ, SEQ)], recv.at[3 + SECT - 1])
    q2_s[...] = split_query(load_query(q_in, g_in, 0))
    peak = jnp.max(scores(0, 0, kk, q2_s, bias, sc), axis=1, keepdims=True)
    arrived(up_s, recv.at[2])

    def attend(step, peak):
        layer, t = SECT - 1 - lax.div(step, TILES), lax.rem(step, TILES)

        @pl.when((t == TILES - 1) & (layer > 0))
        def _():
            arrived(q_in.at[pl.ds((layer - 1) * SEQ, SEQ)], recv.at[2 + layer])

        peak = one_step(step, peak, q_in, g_in, k_in, grad, kk, vt, bias, sc, ex, dp, dkv, q2_s, up_s)

        def send_grad(k, _):
            block = t * GRP + k
            own = (layer == section) & (block == seq)

            @pl.when(own)
            def _():
                keep(grad.at[layer * SEQ + block], acts_out.at[mine, columns(seq)], recv.at[10])

            @pl.when(jnp.logical_not(own))
            def _():
                push(
                    grad.at[layer * SEQ + block], acts_out.at[mine, columns(seq)],
                    send.at[7], recv.at[10], (layer, block),
                )

            return 0

        lax.fori_loop(0, GRP, send_grad, 0)
        return peak

    lax.fori_loop(0, STEPS, attend, peak)

    order = (1 - chip, chip)
    for turn in range(2):
        kv = order[turn]
        far = pl.ds(pl.multiple_of((1 - core) * KHALF, DH), KHALF)
        outgoing[turn] = dkv[kv, :, far].astype(jnp.bfloat16).T
        push(outgoing.at[turn], from_core.at[turn], send.at[8 + turn], recv.at[11 + turn], (sibling, seq))
    near = pl.ds(pl.multiple_of(core * KHALF, DH), KHALF)

    def piece_rows(p):
        return rows_of(lax.rem(lax.div(seq, PBLOCKS) + p, PIECES) * PROWS, PROWS)

    part[0] = dkv[order[0], :, near].T.astype(jnp.bfloat16)
    arrived(from_core.at[0], recv.at[11])
    for p in range(PIECES):
        rows = piece_rows(p)
        part[0, rows] = (part[0, rows].astype(jnp.float32) + from_core[0, rows].astype(jnp.float32)).astype(jnp.bfloat16)
        push(part.at[0, rows], from_chip.at[rows], send.at[10], recv.at[13 + p], (across, seq))
    part[1] = dkv[order[1], :, near].T.astype(jnp.bfloat16)
    arrived(from_core.at[1], recv.at[12])
    k_target = k_out.at[core, :, columns(seq)]
    v_target = v_out.at[core, :, columns(seq)]

    def send_totals(p, target, sem):
        start = lax.rem(lax.div(seq, PBLOCKS) + p, PIECES) * PBLOCKS

        def some(i, _):
            block = start + lax.rem(seq + i, PBLOCKS)
            src = total.at[rows_of(block * HALF, HALF)]

            @pl.when(block == seq)
            def _():
                keep(src, target, sem)

            @pl.when(block != seq)
            def _():
                push(src, target, send.at[11], sem, (section, block))

            push(src, target, send.at[11], sem, (across, block))
            return 0

        lax.fori_loop(0, PBLOCKS, some, 0)

    for p in range(PIECES):
        rows = piece_rows(p)
        arrived(from_chip.at[rows], recv.at[13 + p])
        total[rows] = (
            part[1, rows].astype(jnp.float32) + from_core[1, rows].astype(jnp.float32)
            + from_chip[rows].astype(jnp.float32)
        ).astype(jnp.bfloat16)

        @pl.when(chip == 0)
        def _():
            send_totals(p, k_target, recv.at[17])

        @pl.when(chip == 1)
        def _():
            send_totals(p, v_target, recv.at[20])

    arrived(k_out.at[core], recv.at[17])
    arrived(v_out.at[core], recv.at[20])
    push(k_out.at[core], k_out.at[core], send.at[12], recv.at[18], (sibling, seq))
    push(v_out.at[core], v_out.at[core], send.at[13], recv.at[19], (sibling, seq))
    arrived(acts_out, recv.at[10])
    arrived(k_out.at[1 - core], recv.at[18])
    arrived(v_out.at[1 - core], recv.at[19])

    arrived(k_in.at[: (SEQ - 1) * HALF], send.at[0])
    arrived(v_in.at[: (SEQ - 1) * HALF], send.at[1])
    arrived(up_s.at[: SEQ - 1], send.at[2])
    arrived(q_in.at[: ALL - 1], send.at[3])
    arrived(g_in.at[: SECT - 1], send.at[4])
    arrived(k_half, send.at[5])
    arrived(v_half, send.at[6])
    arrived(grad.at[: ALL - 1], send.at[7])
    arrived(outgoing.at[0], send.at[8])
    arrived(outgoing.at[1], send.at[9])
    arrived(from_chip, send.at[10])
    arrived(k_in.at[: (2 * SEQ - 1) * HALF], send.at[11])
    arrived(k_out.at[core], send.at[12])
    arrived(v_out.at[core], send.at[13])


def attention_grads(offs, acts, top, keys, vals, gain):
    bf = jnp.bfloat16
    any_space = pl.BlockSpec(memory_space=pl.ANY)
    return pl.pallas_call(
        fused_kernel,
        out_shape=(
            jax.ShapeDtypeStruct((SECT * RB, SEQ * DH), bf),
            jax.ShapeDtypeStruct((2, HALF, SEQ * DH), bf),
            jax.ShapeDtypeStruct((2, HALF, SEQ * DH), bf),
        ),
        in_specs=[pl.BlockSpec(memory_space=pltpu.SMEM)] + [any_space] * 5,
        out_specs=(any_space, any_space, any_space),
        scratch_shapes=[
            pltpu.VMEM((ALL, RB, DH), bf),
            pltpu.VMEM((SEQ, RB, DH), bf),
            pltpu.VMEM((KLEN, DH), bf),
            pltpu.VMEM((KLEN, DH), bf),
            pltpu.VMEM((SECT, 8, DH), jnp.float32),
            pltpu.VMEM((ALL, RB, DH), bf),
            pltpu.VMEM((2 * DH, KLEN), bf),
            pltpu.VMEM((DH, KLEN), bf),
            pltpu.VMEM((TILES, TILE, KLEN), jnp.float32),
            pltpu.VMEM((2, TILE, KLEN), jnp.float32),
            pltpu.VMEM((TILE, KLEN), bf),
            pltpu.VMEM((TILE, KLEN), jnp.float32),
            pltpu.VMEM((2, DH, KLEN), jnp.float32),
            pltpu.VMEM((TILE, 2 * DH), bf),
            pltpu.VMEM((2, KHALF, DH), bf),
            pltpu.VMEM((2, KHALF, DH), bf),
            pltpu.VMEM((2, KHALF, DH), bf),
            pltpu.VMEM((KHALF, DH), bf),
            pltpu.VMEM((KHALF, DH), bf),
            pltpu.SemaphoreType.DMA((14,)),
            pltpu.SemaphoreType.DMA((21,)),
            pltpu.SemaphoreType.REGULAR,
        ],
        compiler_params=pltpu.CompilerParams(
            collective_id=0, has_side_effects=True, vmem_limit_bytes=60 * 2**20
        ),
    )(offs, acts, top, keys, vals, gain)


def local(acts, gains, grad_top, keys, values, offsets):
    seq = lax.axis_index("seq")
    gain = jnp.broadcast_to(lax.dynamic_slice(gains, (0, seq * DH), (1, DH)), (8, DH))
    out_acts, out_keys, out_values = attention_grads(
        offsets, acts[0], grad_top, keys.reshape(2, HALF, -1), values.reshape(2, HALF, -1), gain
    )
    return (out_acts[None], out_keys.reshape(2 * HALF, -1), out_values.reshape(2 * HALF, -1))


def solution(mesh):
    return jax.shard_map(
        local,
        mesh=mesh,
        in_specs=(
            P("section", "seq", None),
            P("section", None),
            P("seq", None),
            P("seq", None),
            P("seq", None),
            P(),
        ),
        out_specs=(P("section", "seq", None), P("seq", None), P("seq", None)),
        check_vma=False,
    )
```

```python
import jax
import jax.numpy as jnp
from jax import lax
from jax.experimental import pallas as pl
from jax.experimental.pallas import tpu as pltpu
from jax.sharding import PartitionSpec as P

DH = 128
SECT = 4
SEQ = 32
ALL = SECT * SEQ
RB = 32
HALF = 48
KHALF = SEQ * HALF
KLEN = 2 * KHALF
TILE = 256
GRP = TILE // RB
TILES = SEQ // GRP
STEPS = SECT * TILES
SIDE = KHALF // 2
PBLOCKS = 8
PROWS = PBLOCKS * HALF
SCALE = 1.0 / DH**0.5
LOG2E = 1.4426950408889634
NO_PEAK = -3e38
MESH = pl.DeviceIdType.MESH


def fdot(a, b):
    return lax.dot_general(a, b, (((1,), (0,)), ((), ())), preferred_element_type=jnp.float32)


def push(src, dst, send, recv, device):
    pltpu.make_async_remote_copy(
        src_ref=src, dst_ref=dst, send_sem=send, recv_sem=recv, device_id=device, device_id_type=MESH
    ).start()


def keep(src, dst, sem):
    pltpu.make_async_copy(src, dst, sem).start()


def arrived(ref, sem):
    pltpu.make_async_copy(ref, ref, sem).wait()


def columns(head):
    return pl.ds(pl.multiple_of(head * DH, DH), DH)


def rows_of(start, count):
    return pl.ds(pl.multiple_of(start, 16), count)


def side_of(z):
    return lax.rem(lax.div(z + 1, 2), 2)


def block_at(y, which, side):
    x, later = lax.div(which, 2), lax.rem(which, 2)
    return (x * 2 + y) * 4 + side + later * (3 - 2 * side)


def head_at(section, seq):
    return lax.div(seq, 4) * 4 + lax.div(section, 2) * 2 + lax.div(lax.rem(seq, 4), 2)


def group_at(section, seq):
    return lax.rem(seq, 2) * 2 + lax.rem(section, 2)


def fill_bias(offs, first, bias):
    sub = lax.broadcasted_iota(jnp.int32, (RB, 1), 0)
    wide = 512

    def tile_bias(t, _):
        def some(j, _):
            flat = lax.broadcasted_iota(jnp.int32, (1, wide), 1) + j * wide
            half, side = lax.div(flat, KHALF), lax.rem(lax.div(flat, SIDE), 2)
            inside = lax.rem(flat, SIDE)
            which = lax.div(inside, HALF)
            block = block_at(lax.div(which, 8), lax.rem(which, 8), side)
            spot = block * (2 * HALF) + half * HALF + lax.rem(inside, HALF)
            cols = pl.ds(pl.multiple_of(j * wide, wide), wide)
            for k in range(GRP):
                qpos = sub + (first + offs[t * GRP + k])
                bias[t, k * RB : (k + 1) * RB, cols] = jnp.where(spot <= qpos, 0.0, -1e30)
            return 0

        lax.fori_loop(0, KLEN // wide, some, 0)
        return 0

    lax.fori_loop(0, TILES, tile_bias, 0)


def load_query(q_in, gains, step):
    layer, t = SECT - 1 - lax.div(step, TILES), lax.rem(step, TILES)
    q = q_in[pl.ds(layer * SEQ + t * GRP, GRP)].reshape(TILE, DH)
    return (q.astype(jnp.float32) * gains[layer][0:1, :]).astype(jnp.bfloat16)


def split_query(q):
    scaled = q.astype(jnp.float32) * (SCALE * LOG2E)
    high = scaled.astype(jnp.bfloat16)
    low = (scaled - high.astype(jnp.float32)).astype(jnp.bfloat16)
    return jnp.concatenate([high, low], axis=1)


def scores(t, slot, kk, q2_s, bias, sc):
    s = fdot(q2_s[...], kk[...]) + bias[t]
    sc[slot] = s
    peak = jnp.full((TILE, DH), NO_PEAK, jnp.float32)
    for c in range(KLEN // DH):
        peak = jnp.maximum(peak, s[:, c * DH : (c + 1) * DH])
    return peak


def one_step(step, peak, q_in, gains, k_in, grad, kk, vt, bias, sc, ex, dp, dkv, q2_s, up_s):
    layer, t = SECT - 1 - lax.div(step, TILES), lax.rem(step, TILES)
    after = jnp.minimum(step + 1, STEPS - 1)
    slot = lax.rem(step, 2)
    up_now = up_s[pl.ds(t * GRP, GRP)].reshape(TILE, DH)
    q2_s[...] = split_query(load_query(q_in, gains, after))
    norm = jnp.zeros((TILE, DH), jnp.float32)
    delta = jnp.zeros((TILE, DH), jnp.float32)
    d = fdot(up_now, vt[...])
    e = jnp.exp2(sc[slot] - peak)
    dp[...] = d
    ex[...] = e.astype(jnp.bfloat16)
    ed = e * d
    for c in range(KLEN // DH):
        norm = norm + e[:, c * DH : (c + 1) * DH]
        delta = delta + ed[:, c * DH : (c + 1) * DH]
    peak_after = scores(lax.rem(after, TILES), 1 - slot, kk, q2_s, bias, sc)
    inv = 1.0 / jnp.sum(norm, axis=1, keepdims=True)
    delta = jnp.sum(delta, axis=1, keepdims=True) * inv
    q = load_query(q_in, gains, step)
    qn = (q.astype(jnp.float32) * (inv * SCALE)).T.astype(jnp.bfloat16)
    un = (up_now.astype(jnp.float32) * inv).T.astype(jnp.bfloat16)
    e = ex[...]
    ds = e * (dp[...] - delta).astype(jnp.bfloat16)
    dq = fdot(ds, k_in[...])
    dkv[0] += fdot(qn, ds)
    dkv[1] += fdot(un, e)
    up = (up_now.astype(jnp.float32) + gains[layer][0:1, :] * (dq * (inv * SCALE))).astype(jnp.bfloat16)
    up = up.reshape(GRP, RB, DH)
    up_s[pl.ds(t * GRP, GRP)] = up
    grad[pl.ds(layer * SEQ + t * GRP, GRP)] = up
    return jnp.max(peak_after, axis=1, keepdims=True)


def fused_kernel(
    offs, acts, top, keys, vals, gain, acts_out, k_out, v_out,
    q_in, up_s, k_in, v_in, g_in, grad, kk, vt, bias, sc, ex, dp, dkv, q2_s,
    outgoing, from_core, part, from_chip, total, send, recv, ready,
):
    section, seq = lax.axis_index("section"), lax.axis_index("seq")
    core, chip = lax.rem(section, 2), lax.div(section, 2)
    sibling = section + 1 - 2 * core
    across = section + 2 - 4 * chip
    me = section * SEQ + seq
    head, group = head_at(section, seq), group_at(section, seq)
    partner = seq + 1 - 2 * lax.rem(seq, 2)
    x, y, z = lax.div(seq, 8), lax.rem(lax.div(seq, 4), 2), lax.rem(seq, 4)
    side = side_of(z)
    mine = rows_of(group * RB, RB)

    barrier = pltpu.get_barrier_semaphore()

    def hello(i, _):
        pl.semaphore_signal(barrier, inc=1, device_id=(section, lax.rem(seq + i, SEQ)), device_id_type=MESH)
        return 0

    lax.fori_loop(1, SEQ, hello, 0)
    for j in range(1, SECT):
        pl.semaphore_signal(barrier, inc=1, device_id=(lax.rem(section + j, SECT), seq), device_id_type=MESH)
    fill_bias(offs, group * RB, bias)
    dkv[...] = jnp.zeros_like(dkv)
    pl.semaphore_wait(barrier, SEQ + SECT - 2)
    for j in range(1, SECT):
        pl.semaphore_signal(ready, inc=1, device_id=(lax.rem(section + j, SECT), seq), device_id_type=MESH)

    here = rows_of(core * KHALF + side * SIDE + (y * 8 + x * 2 + lax.div(z, 2)) * HALF, HALF)
    k_here, v_here = k_in.at[here], v_in.at[here]

    def send_cached(i, _):
        to = lax.rem(seq + i, SEQ)
        there = head_at(section, to)
        push(keys.at[core, :, columns(there)], k_here, send.at[0], recv.at[0], (section, to))
        push(vals.at[core, :, columns(there)], v_here, send.at[1], recv.at[1], (section, to))
        return 0

    def query_rows(to_section, to):
        return acts.at[rows_of(group_at(to_section, to) * RB, RB), columns(head_at(to_section, to))]

    def send_query(to_section, to):
        push(query_rows(to_section, to), q_in.at[me], send.at[3], recv.at[3 + section], (to_section, to))

    def send_queries():
        for j in range(1, SECT):
            send_query(lax.rem(section + j, SECT), seq)

        def some(i, _):
            for j in range(SECT):
                send_query(lax.rem(section + j, SECT), lax.rem(seq + i, SEQ))
            return 0

        lax.fori_loop(1, SEQ, some, 0)

    def top_rows(to):
        return top.at[rows_of(group_at(section, to) * RB, RB), columns(head_at(section, to))]

    def send_top(i, _):
        to = lax.rem(seq + i, SEQ)
        push(top_rows(to), up_s.at[seq], send.at[2], recv.at[2], (section, to))
        return 0

    keep(keys.at[core, :, columns(head)], k_here, recv.at[0])
    keep(vals.at[core, :, columns(head)], v_here, recv.at[1])
    keep(top_rows(seq), up_s.at[seq], recv.at[2])
    keep(query_rows(section, seq), q_in.at[me], recv.at[3 + section])
    keep(gain.at[chip], g_in.at[section], recv.at[7])
    pl.semaphore_wait(ready, SECT - 1)

    @pl.when(section == SECT - 1)
    def _():
        send_queries()

    lax.fori_loop(1, SEQ, send_cached, 0)
    for j in range(1, SECT):
        to_section = lax.rem(section + j, SECT)
        push(gain.at[lax.div(to_section, 2)], g_in.at[section], send.at[4], recv.at[7], (to_section, seq))
    lax.fori_loop(1, SEQ, send_top, 0)
    k_half, v_half = k_in.at[rows_of(core * KHALF, KHALF)], v_in.at[rows_of(core * KHALF, KHALF)]
    k_other, v_other = k_in.at[rows_of((1 - core) * KHALF, KHALF)], v_in.at[rows_of((1 - core) * KHALF, KHALF)]
    arrived(k_half, recv.at[0])
    push(k_half, k_half, send.at[5], recv.at[8], (sibling, seq))
    arrived(v_half, recv.at[1])
    push(v_half, v_half, send.at[6], recv.at[9], (sibling, seq))

    @pl.when(section != SECT - 1)
    def _():
        send_queries()

    arrived(k_other, recv.at[8])
    kt = k_in[...].T
    kk[:DH, :] = kt
    kk[DH:, :] = kt
    arrived(v_other, recv.at[9])
    vt[...] = v_in[...].T
    arrived(g_in, recv.at[7])
    arrived(q_in.at[pl.ds((SECT - 1) * SEQ, SEQ)], recv.at[3 + SECT - 1])
    q2_s[...] = split_query(load_query(q_in, g_in, 0))
    peak = jnp.max(scores(0, 0, kk, q2_s, bias, sc), axis=1, keepdims=True)
    arrived(up_s, recv.at[2])

    def attend(step, peak):
        layer, t = SECT - 1 - lax.div(step, TILES), lax.rem(step, TILES)

        @pl.when((t == TILES - 1) & (layer > 0))
        def _():
            arrived(q_in.at[pl.ds((layer - 1) * SEQ, SEQ)], recv.at[2 + layer])

        peak = one_step(step, peak, q_in, g_in, k_in, grad, kk, vt, bias, sc, ex, dp, dkv, q2_s, up_s)

        def send_grad(k, _):
            block = t * GRP + k
            own = (layer == section) & (block == seq)

            @pl.when(own)
            def _():
                keep(grad.at[layer * SEQ + block], acts_out.at[mine, columns(head)], recv.at[10])

            @pl.when(jnp.logical_not(own))
            def _():
                push(
                    grad.at[layer * SEQ + block], acts_out.at[mine, columns(head)],
                    send.at[7], recv.at[10], (layer, block),
                )

            return 0

        lax.fori_loop(0, GRP, send_grad, 0)
        return peak

    lax.fori_loop(0, STEPS, attend, peak)

    near_half = pl.ds(pl.multiple_of(core * KHALF, DH), KHALF)
    far_half = pl.ds(pl.multiple_of((1 - core) * KHALF, DH), KHALF)
    for kv in range(2):
        outgoing[kv] = dkv[kv, :, far_half].astype(jnp.bfloat16).T
        push(outgoing.at[kv], from_core.at[kv], send.at[8 + kv], recv.at[11 + kv], (sibling, seq))

    def add_core(kv, rows):
        return part[kv, rows].astype(jnp.float32) + from_core[kv, rows].astype(jnp.float32)

    def piece(p):
        return lax.rem(y + p, 2) * PROWS

    for kv in range(2):
        part[kv] = dkv[kv, :, near_half].astype(jnp.bfloat16).T
        arrived(from_core.at[kv], recv.at[11 + kv])
        for p in range(2):
            rows = rows_of((1 - side) * SIDE + piece(p), PROWS)
            part[kv, rows] = add_core(kv, rows).astype(jnp.bfloat16)
            push(
                part.at[kv, rows], from_chip.at[kv, rows_of(piece(p), PROWS)],
                send.at[10], recv.at[13 + 2 * kv + p], (section, partner),
            )

    def send_totals(kv, p, target):
        def some(i, _):
            which = lax.rem(2 * x + i, PBLOCKS)
            block = block_at(lax.rem(y + p, 2), which, side)
            src = total.at[kv, rows_of(piece(p) + which * HALF, HALF)]

            @pl.when(block == seq)
            def _():
                keep(src, target, recv.at[17 + kv])

            @pl.when(block != seq)
            def _():
                push(src, target, send.at[11 + kv], recv.at[17 + kv], (section, block))

            push(src, target, send.at[11 + kv], recv.at[17 + kv], (across, block))
            return 0

        lax.fori_loop(0, PBLOCKS, some, 0)

    for kv, out in ((0, k_out), (1, v_out)):
        for p in range(2):
            done = rows_of(piece(p), PROWS)
            arrived(from_chip.at[kv, done], recv.at[13 + 2 * kv + p])
            total[kv, done] = (
                add_core(kv, rows_of(side * SIDE + piece(p), PROWS)) + from_chip[kv, done].astype(jnp.float32)
            ).astype(jnp.bfloat16)
            send_totals(kv, p, out.at[core, :, columns(head)])

    for kv, out in ((0, k_out), (1, v_out)):
        arrived(out.at[core], recv.at[17 + kv])
        push(out.at[core], out.at[core], send.at[13 + kv], recv.at[19 + kv], (sibling, seq))
    arrived(acts_out, recv.at[10])
    for kv, out in ((0, k_out), (1, v_out)):
        arrived(out.at[1 - core], recv.at[19 + kv])

    arrived(k_in.at[: (SEQ - 1) * HALF], send.at[0])
    arrived(v_in.at[: (SEQ - 1) * HALF], send.at[1])
    arrived(up_s.at[: SEQ - 1], send.at[2])
    arrived(q_in.at[: ALL - 1], send.at[3])
    arrived(g_in.at[: SECT - 1], send.at[4])
    arrived(k_half, send.at[5])
    arrived(v_half, send.at[6])
    arrived(grad.at[: ALL - 1], send.at[7])
    arrived(from_chip, send.at[10])
    for kv, out in ((0, k_out), (1, v_out)):
        arrived(outgoing.at[kv], send.at[8 + kv])
        arrived(k_in.at[: (SEQ - 1) * HALF], send.at[11 + kv])
        arrived(out.at[core], send.at[13 + kv])


def attention_grads(offs, acts, top, keys, vals, gain):
    bf = jnp.bfloat16
    any_space = pl.BlockSpec(memory_space=pl.ANY)
    return pl.pallas_call(
        fused_kernel,
        out_shape=(
            jax.ShapeDtypeStruct((SECT * RB, SEQ * DH), bf),
            jax.ShapeDtypeStruct((2, HALF, SEQ * DH), bf),
            jax.ShapeDtypeStruct((2, HALF, SEQ * DH), bf),
        ),
        in_specs=[pl.BlockSpec(memory_space=pltpu.SMEM)] + [any_space] * 5,
        out_specs=(any_space, any_space, any_space),
        scratch_shapes=[
            pltpu.VMEM((ALL, RB, DH), bf),
            pltpu.VMEM((SEQ, RB, DH), bf),
            pltpu.VMEM((KLEN, DH), bf),
            pltpu.VMEM((KLEN, DH), bf),
            pltpu.VMEM((SECT, 8, DH), jnp.float32),
            pltpu.VMEM((ALL, RB, DH), bf),
            pltpu.VMEM((2 * DH, KLEN), bf),
            pltpu.VMEM((DH, KLEN), bf),
            pltpu.VMEM((TILES, TILE, KLEN), jnp.float32),
            pltpu.VMEM((2, TILE, KLEN), jnp.float32),
            pltpu.VMEM((TILE, KLEN), bf),
            pltpu.VMEM((TILE, KLEN), jnp.float32),
            pltpu.VMEM((2, DH, KLEN), jnp.float32),
            pltpu.VMEM((TILE, 2 * DH), bf),
            pltpu.VMEM((2, KHALF, DH), bf),
            pltpu.VMEM((2, KHALF, DH), bf),
            pltpu.VMEM((2, KHALF, DH), bf),
            pltpu.VMEM((2, SIDE, DH), bf),
            pltpu.VMEM((2, SIDE, DH), bf),
            pltpu.SemaphoreType.DMA((15,)),
            pltpu.SemaphoreType.DMA((21,)),
            pltpu.SemaphoreType.REGULAR,
        ],
        compiler_params=pltpu.CompilerParams(
            collective_id=0, has_side_effects=True, vmem_limit_bytes=60 * 2**20
        ),
    )(offs, acts, top, keys, vals, gain)


def local(acts, gains, grad_top, keys, values, offsets):
    low_head = head_at(0, lax.axis_index("seq"))
    slices = [lax.dynamic_slice(gains, (0, (low_head + step) * DH), (1, DH)) for step in (0, 2)]
    gain = jnp.broadcast_to(jnp.stack(slices), (2, 8, DH))
    out_acts, out_keys, out_values = attention_grads(
        offsets, acts[0], grad_top, keys.reshape(2, HALF, -1), values.reshape(2, HALF, -1), gain
    )
    return (out_acts[None], out_keys.reshape(2 * HALF, -1), out_values.reshape(2 * HALF, -1))


def solution(mesh):
    return jax.shard_map(
        local,
        mesh=mesh,
        in_specs=(
            P("section", "seq", None),
            P("section", None),
            P("seq", None),
            P("seq", None),
            P("seq", None),
            P(),
        ),
        out_specs=(P("section", "seq", None), P("seq", None), P("seq", None)),
        check_vma=False,
    )
```

```python
import jax
import jax.numpy as jnp
from jax import lax
from jax.experimental import pallas as pl
from jax.experimental.pallas import tpu as pltpu
from jax.sharding import PartitionSpec as P

DH = 128
SECT = 4
SEQ = 32
ALL = SECT * SEQ
RB = 32
HALF = 48
KHALF = SEQ * HALF
KLEN = 2 * KHALF
TILE = 256
GRP = TILE // RB
TILES = SEQ // GRP
STEPS = SECT * TILES
SIDE = KHALF // 2
PBLOCKS = 8
PROWS = PBLOCKS * HALF
SCALE = 1.0 / DH**0.5
LOG2E = 1.4426950408889634
NO_PEAK = -3e38
MESH = pl.DeviceIdType.MESH


def fdot(a, b):
    return lax.dot_general(a, b, (((1,), (0,)), ((), ())), preferred_element_type=jnp.float32)


def push(src, dst, send, recv, device):
    pltpu.make_async_remote_copy(
        src_ref=src, dst_ref=dst, send_sem=send, recv_sem=recv, device_id=device, device_id_type=MESH
    ).start()


def keep(src, dst, sem):
    pltpu.make_async_copy(src, dst, sem).start()


def arrived(ref, sem):
    pltpu.make_async_copy(ref, ref, sem).wait()


def columns(head):
    return pl.ds(pl.multiple_of(head * DH, DH), DH)


def rows_of(start, count):
    return pl.ds(pl.multiple_of(start, 16), count)


def side_of(z):
    return lax.rem(lax.div(z + 1, 2), 2)


def block_at(y, which, side):
    x, later = lax.div(which, 2), lax.rem(which, 2)
    return (x * 2 + y) * 4 + side + later * (3 - 2 * side)


def head_at(section, seq):
    return lax.div(seq, 4) * 4 + lax.div(section, 2) * 2 + lax.div(lax.rem(seq, 4), 2)


def group_at(section, seq):
    return lax.rem(seq, 2) * 2 + lax.rem(section, 2)


def fill_bias(offs, first, bias):
    sub = lax.broadcasted_iota(jnp.int32, (RB, 1), 0)
    wide = 512

    def tile_bias(t, _):
        def some(j, _):
            flat = lax.broadcasted_iota(jnp.int32, (1, wide), 1) + j * wide
            half, side = lax.div(flat, KHALF), lax.rem(lax.div(flat, SIDE), 2)
            inside = lax.rem(flat, SIDE)
            which = lax.div(inside, HALF)
            block = block_at(lax.div(which, 8), lax.rem(which, 8), side)
            spot = block * (2 * HALF) + half * HALF + lax.rem(inside, HALF)
            cols = pl.ds(pl.multiple_of(j * wide, wide), wide)
            for k in range(GRP):
                qpos = sub + (first + offs[t * GRP + k])
                bias[t, k * RB : (k + 1) * RB, cols] = jnp.where(spot <= qpos, 0.0, -1e30)
            return 0

        lax.fori_loop(0, KLEN // wide, some, 0)
        return 0

    lax.fori_loop(0, TILES, tile_bias, 0)


def at_step(step, turn):
    return SECT - 1 - lax.div(step, TILES), lax.rem(step + turn, TILES)


def load_query(q_in, gains, step, turn):
    layer, t = at_step(step, turn)
    q = q_in[pl.ds(layer * SEQ + t * GRP, GRP)].reshape(TILE, DH)
    return (q.astype(jnp.float32) * gains[layer][0:1, :]).astype(jnp.bfloat16)


def split_query(q):
    scaled = q.astype(jnp.float32) * (SCALE * LOG2E)
    high = scaled.astype(jnp.bfloat16)
    low = (scaled - high.astype(jnp.float32)).astype(jnp.bfloat16)
    return jnp.concatenate([high, low], axis=1)


def scores(t, slot, kk, q2_s, bias, sc):
    s = fdot(q2_s[...], kk[...]) + bias[t]
    sc[slot] = s
    peak = jnp.full((TILE, DH), NO_PEAK, jnp.float32)
    for c in range(KLEN // DH):
        peak = jnp.maximum(peak, s[:, c * DH : (c + 1) * DH])
    return peak


def one_step(step, turn, peak, q_in, gains, k_in, grad, kk, vt, bias, sc, ex, dp, dkv, q2_s, up_s):
    layer, t = at_step(step, turn)
    after = jnp.minimum(step + 1, STEPS - 1)
    slot = lax.rem(step, 2)
    up_now = up_s[pl.ds(t * GRP, GRP)].reshape(TILE, DH)
    q2_s[...] = split_query(load_query(q_in, gains, after, turn))
    norm = jnp.zeros((TILE, DH), jnp.float32)
    delta = jnp.zeros((TILE, DH), jnp.float32)
    d = fdot(up_now, vt[...])
    e = jnp.exp2(sc[slot] - peak)
    dp[...] = d
    ex[...] = e.astype(jnp.bfloat16)
    ed = e * d
    for c in range(KLEN // DH):
        norm = norm + e[:, c * DH : (c + 1) * DH]
        delta = delta + ed[:, c * DH : (c + 1) * DH]
    peak_after = scores(at_step(after, turn)[1], 1 - slot, kk, q2_s, bias, sc)
    inv = 1.0 / jnp.sum(norm, axis=1, keepdims=True)
    delta = jnp.sum(delta, axis=1, keepdims=True) * inv
    q = load_query(q_in, gains, step, turn)
    qn = (q.astype(jnp.float32) * (inv * SCALE)).T.astype(jnp.bfloat16)
    un = (up_now.astype(jnp.float32) * inv).T.astype(jnp.bfloat16)
    e = ex[...]
    ds = e * (dp[...] - delta).astype(jnp.bfloat16)
    dq = fdot(ds, k_in[...])
    dkv[0] += fdot(qn, ds)
    dkv[1] += fdot(un, e)
    up = (up_now.astype(jnp.float32) + gains[layer][0:1, :] * (dq * (inv * SCALE))).astype(jnp.bfloat16)
    up = up.reshape(GRP, RB, DH)
    up_s[pl.ds(t * GRP, GRP)] = up
    grad[pl.ds(layer * SEQ + t * GRP, GRP)] = up
    return jnp.max(peak_after, axis=1, keepdims=True)


def fused_kernel(
    offs, acts, top, keys, vals, gains, acts_out, k_out, v_out,
    q_in, up_s, k_in, v_in, g_in, grad, kk, vt, bias, sc, ex, dp, dkv, q2_s,
    outgoing, from_core, part, from_chip, total, gain, send, recv, ready,
):
    section, seq = lax.axis_index("section"), lax.axis_index("seq")
    core, chip = lax.rem(section, 2), lax.div(section, 2)
    sibling = section + 1 - 2 * core
    across = section + 2 - 4 * chip
    me = section * SEQ + seq
    head, group = head_at(section, seq), group_at(section, seq)
    partner = seq + 1 - 2 * lax.rem(seq, 2)
    x, y, z = lax.div(seq, 8), lax.rem(lax.div(seq, 4), 2), lax.rem(seq, 4)
    side = side_of(z)
    turn = lax.rem(x + z, TILES)
    mine = rows_of(group * RB, RB)

    barrier = pltpu.get_barrier_semaphore()

    def hello(i, _):
        pl.semaphore_signal(barrier, inc=1, device_id=(section, lax.rem(seq + i, SEQ)), device_id_type=MESH)
        return 0

    lax.fori_loop(1, SEQ, hello, 0)
    for j in range(1, SECT):
        pl.semaphore_signal(barrier, inc=1, device_id=(lax.rem(section + j, SECT), seq), device_id_type=MESH)
    for up in range(2):
        gain[up] = jnp.broadcast_to(gains[:, columns(head_at(2 * up, seq))], (8, DH))
    fill_bias(offs, group * RB, bias)
    dkv[...] = jnp.zeros_like(dkv)
    pl.semaphore_wait(barrier, SEQ + SECT - 2)
    for j in range(1, SECT):
        pl.semaphore_signal(ready, inc=1, device_id=(lax.rem(section + j, SECT), seq), device_id_type=MESH)

    here = rows_of(core * KHALF + side * SIDE + (y * 8 + x * 2 + lax.div(z, 2)) * HALF, HALF)
    k_here, v_here = k_in.at[here], v_in.at[here]

    def send_cached(i, _):
        to = lax.rem(seq + i, SEQ)
        there = head_at(section, to)
        push(keys.at[core, :, columns(there)], k_here, send.at[0], recv.at[0], (section, to))
        push(vals.at[core, :, columns(there)], v_here, send.at[1], recv.at[1], (section, to))
        return 0

    def query_rows(to_section, to):
        return acts.at[rows_of(group_at(to_section, to) * RB, RB), columns(head_at(to_section, to))]

    def send_query(to_section, to):
        push(query_rows(to_section, to), q_in.at[me], send.at[3], recv.at[3 + section], (to_section, to))

    def send_queries():
        for j in range(1, SECT):
            send_query(lax.rem(section + j, SECT), seq)

        def some(i, _):
            for j in range(SECT):
                send_query(lax.rem(section + j, SECT), lax.rem(seq + i, SEQ))
            return 0

        lax.fori_loop(1, SEQ, some, 0)

    def top_rows(to):
        return top.at[rows_of(group_at(section, to) * RB, RB), columns(head_at(section, to))]

    def send_top(i, _):
        to = lax.rem(seq + i, SEQ)
        push(top_rows(to), up_s.at[seq], send.at[2], recv.at[2], (section, to))
        return 0

    keep(keys.at[core, :, columns(head)], k_here, recv.at[0])
    keep(vals.at[core, :, columns(head)], v_here, recv.at[1])
    keep(top_rows(seq), up_s.at[seq], recv.at[2])
    keep(query_rows(section, seq), q_in.at[me], recv.at[3 + section])
    keep(gain.at[chip], g_in.at[section], recv.at[7])
    pl.semaphore_wait(ready, SECT - 1)

    lax.fori_loop(1, SEQ, send_cached, 0)
    @pl.when(section == SECT - 1)
    def _():
        send_queries()

    for j in range(1, SECT):
        to_section = lax.rem(section + j, SECT)
        push(gain.at[lax.div(to_section, 2)], g_in.at[section], send.at[4], recv.at[7], (to_section, seq))
    lax.fori_loop(1, SEQ, send_top, 0)
    k_half, v_half = k_in.at[rows_of(core * KHALF, KHALF)], v_in.at[rows_of(core * KHALF, KHALF)]
    k_other, v_other = k_in.at[rows_of((1 - core) * KHALF, KHALF)], v_in.at[rows_of((1 - core) * KHALF, KHALF)]
    arrived(k_half, recv.at[0])
    push(k_half, k_half, send.at[5], recv.at[8], (sibling, seq))
    arrived(v_half, recv.at[1])
    push(v_half, v_half, send.at[6], recv.at[9], (sibling, seq))

    @pl.when(section != SECT - 1)
    def _():
        send_queries()

    arrived(k_other, recv.at[8])
    kt = k_in[...].T
    kk[:DH, :] = kt
    kk[DH:, :] = kt
    arrived(v_other, recv.at[9])
    vt[...] = v_in[...].T
    arrived(g_in, recv.at[7])
    arrived(q_in.at[pl.ds((SECT - 1) * SEQ, SEQ)], recv.at[3 + SECT - 1])
    q2_s[...] = split_query(load_query(q_in, g_in, 0, turn))
    peak = jnp.max(scores(turn, 0, kk, q2_s, bias, sc), axis=1, keepdims=True)
    arrived(up_s, recv.at[2])

    def send_grads(step):
        layer, t = at_step(step, turn)
        first = layer * SEQ + t * GRP

        def send_one(inside):
            push(
                grad.at[first + inside], acts_out.at[mine, columns(head)],
                send.at[7], recv.at[10], (layer, t * GRP + inside),
            )

        for k in range(1, GRP):
            send_one(lax.rem(seq + k, GRP))
        inside = lax.rem(seq, GRP)
        own = (layer == section) & (t == lax.div(seq, GRP))

        @pl.when(own)
        def _():
            keep(grad.at[first + inside], acts_out.at[mine, columns(head)], recv.at[10])

        @pl.when(jnp.logical_not(own))
        def _():
            send_one(inside)

    def attend(step, peak):
        layer = SECT - 1 - lax.div(step, TILES)

        @pl.when((lax.rem(step, TILES) == TILES - 1) & (layer > 0))
        def _():
            arrived(q_in.at[pl.ds((layer - 1) * SEQ, SEQ)], recv.at[2 + layer])

        return one_step(step, turn, peak, q_in, g_in, k_in, grad, kk, vt, bias, sc, ex, dp, dkv, q2_s, up_s)

    def attend_send(step, peak):
        peak = attend(step, peak)
        send_grads(step)
        return peak

    lax.fori_loop(0, STEPS, attend_send, peak)

    near_half = pl.ds(pl.multiple_of(core * KHALF, DH), KHALF)
    far_half = pl.ds(pl.multiple_of((1 - core) * KHALF, DH), KHALF)
    for kv in range(2):
        outgoing[kv] = dkv[kv, :, far_half].astype(jnp.bfloat16).T
        push(outgoing.at[kv], from_core.at[kv], send.at[8 + kv], recv.at[11 + kv], (sibling, seq))

    def add_core(kv, rows):
        return part[kv, rows].astype(jnp.float32) + from_core[kv, rows].astype(jnp.float32)

    def piece(p):
        return lax.rem(y + p, 2) * PROWS

    for kv in range(2):
        part[kv] = dkv[kv, :, near_half].astype(jnp.bfloat16).T
        arrived(from_core.at[kv], recv.at[11 + kv])
        for p in range(2):
            rows = rows_of((1 - side) * SIDE + piece(p), PROWS)
            part[kv, rows] = add_core(kv, rows).astype(jnp.bfloat16)
            push(
                part.at[kv, rows], from_chip.at[kv, rows_of(piece(p), PROWS)],
                send.at[10], recv.at[13 + 2 * kv + p], (section, partner),
            )

    def send_totals(kv, p, target):
        def some(i, _):
            which = lax.rem(2 * (x + z) + section + i, PBLOCKS)
            block = block_at(lax.rem(y + p, 2), which, side)
            src = total.at[kv, rows_of(piece(p) + which * HALF, HALF)]

            @pl.when(block == seq)
            def _():
                keep(src, target, recv.at[17 + kv])

            @pl.when(block != seq)
            def _():
                push(src, target, send.at[11 + kv], recv.at[17 + kv], (section, block))

            push(src, target, send.at[11 + kv], recv.at[17 + kv], (across, block))
            return 0

        lax.fori_loop(0, PBLOCKS, some, 0)

    for kv, out in ((0, k_out), (1, v_out)):
        for p in range(2):
            done = rows_of(piece(p), PROWS)
            arrived(from_chip.at[kv, done], recv.at[13 + 2 * kv + p])
            total[kv, done] = (
                add_core(kv, rows_of(side * SIDE + piece(p), PROWS)) + from_chip[kv, done].astype(jnp.float32)
            ).astype(jnp.bfloat16)
            send_totals(kv, p, out.at[core, :, columns(head)])

    for kv, out in ((0, k_out), (1, v_out)):
        arrived(out.at[core], recv.at[17 + kv])
        push(out.at[core], out.at[core], send.at[13 + kv], recv.at[19 + kv], (sibling, seq))
    arrived(acts_out, recv.at[10])
    for kv, out in ((0, k_out), (1, v_out)):
        arrived(out.at[1 - core], recv.at[19 + kv])

    arrived(k_in.at[: (SEQ - 1) * HALF], send.at[0])
    arrived(v_in.at[: (SEQ - 1) * HALF], send.at[1])
    arrived(up_s.at[: SEQ - 1], send.at[2])
    arrived(q_in.at[: ALL - 1], send.at[3])
    arrived(g_in.at[: SECT - 1], send.at[4])
    arrived(k_half, send.at[5])
    arrived(v_half, send.at[6])
    arrived(grad.at[: ALL - 1], send.at[7])
    arrived(from_chip, send.at[10])
    for kv, out in ((0, k_out), (1, v_out)):
        arrived(outgoing.at[kv], send.at[8 + kv])
        arrived(k_in.at[: (SEQ - 1) * HALF], send.at[11 + kv])
        arrived(out.at[core], send.at[13 + kv])


def attention_grads(offs, acts, top, keys, vals, gains):
    bf = jnp.bfloat16
    any_space = pl.BlockSpec(memory_space=pl.ANY)
    return pl.pallas_call(
        fused_kernel,
        out_shape=(
            jax.ShapeDtypeStruct((SECT * RB, SEQ * DH), bf),
            jax.ShapeDtypeStruct((2, HALF, SEQ * DH), bf),
            jax.ShapeDtypeStruct((2, HALF, SEQ * DH), bf),
        ),
        in_specs=[pl.BlockSpec(memory_space=pltpu.SMEM)] + [any_space] * 4 + [pl.BlockSpec(memory_space=pltpu.VMEM)],
        out_specs=(any_space, any_space, any_space),
        scratch_shapes=[
            pltpu.VMEM((ALL, RB, DH), bf),
            pltpu.VMEM((SEQ, RB, DH), bf),
            pltpu.VMEM((KLEN, DH), bf),
            pltpu.VMEM((KLEN, DH), bf),
            pltpu.VMEM((SECT, 8, DH), jnp.float32),
            pltpu.VMEM((ALL, RB, DH), bf),
            pltpu.VMEM((2 * DH, KLEN), bf),
            pltpu.VMEM((DH, KLEN), bf),
            pltpu.VMEM((TILES, TILE, KLEN), jnp.float32),
            pltpu.VMEM((2, TILE, KLEN), jnp.float32),
            pltpu.VMEM((TILE, KLEN), bf),
            pltpu.VMEM((TILE, KLEN), jnp.float32),
            pltpu.VMEM((2, DH, KLEN), jnp.float32),
            pltpu.VMEM((TILE, 2 * DH), bf),
            pltpu.VMEM((2, KHALF, DH), bf),
            pltpu.VMEM((2, KHALF, DH), bf),
            pltpu.VMEM((2, KHALF, DH), bf),
            pltpu.VMEM((2, SIDE, DH), bf),
            pltpu.VMEM((2, SIDE, DH), bf),
            pltpu.VMEM((2, 8, DH), jnp.float32),
            pltpu.SemaphoreType.DMA((15,)),
            pltpu.SemaphoreType.DMA((21,)),
            pltpu.SemaphoreType.REGULAR,
        ],
        compiler_params=pltpu.CompilerParams(
            collective_id=0, has_side_effects=True, vmem_limit_bytes=60 * 2**20
        ),
    )(offs, acts, top, keys, vals, gains)


def store_kernel(a, b, c, a_out, b_out, c_out, sems):
    copies = [
        pltpu.make_async_copy(src, dst, sems.at[i])
        for i, (src, dst) in enumerate(((a, a_out), (b, b_out), (c, c_out)))
    ]
    for copy in copies:
        copy.start()
    for copy in copies:
        copy.wait()


def store(*arrays):
    any_space = pl.BlockSpec(memory_space=pl.ANY)
    return pl.pallas_call(
        store_kernel,
        out_shape=tuple(jax.ShapeDtypeStruct(a.shape, a.dtype) for a in arrays),
        in_specs=[pl.BlockSpec(memory_space=pltpu.VMEM)] * 3,
        out_specs=(any_space,) * 3,
        scratch_shapes=[pltpu.SemaphoreType.DMA((3,))],
    )(*arrays)


def local(acts, gains, grad_top, keys, values, offsets):
    out_acts, out_keys, out_values = attention_grads(
        offsets, acts[0], grad_top, keys.reshape(2, HALF, -1), values.reshape(2, HALF, -1), gains
    )
    out_acts, out_keys, out_values = store(out_acts, out_keys, out_values)
    return (out_acts[None], out_keys.reshape(2 * HALF, -1), out_values.reshape(2 * HALF, -1))


def solution(mesh):
    return jax.shard_map(
        local,
        mesh=mesh,
        in_specs=(
            P("section", "seq", None),
            P("section", None),
            P("seq", None),
            P("seq", None),
            P("seq", None),
            P(),
        ),
        out_specs=(P("section", "seq", None), P("seq", None), P("seq", None)),
        check_vma=False,
    )
```

```python
import jax
import jax.numpy as jnp
from jax import lax
from jax.experimental import pallas as pl
from jax.experimental.pallas import tpu as pltpu
from jax.sharding import PartitionSpec as P

DH = 128
SECT = 4
SEQ = 32
ALL = SECT * SEQ
RB = 32
HALF = 48
KHALF = SEQ * HALF
KLEN = 2 * KHALF
TILE = 256
GRP = TILE // RB
TILES = SEQ // GRP
STEPS = SECT * TILES
SIDE = KHALF // 2
PBLOCKS = 8
PROWS = PBLOCKS * HALF
SCALE = 1.0 / DH**0.5
LOG2E = 1.4426950408889634
NO_PEAK = -3e38
MESH = pl.DeviceIdType.MESH


def fdot(a, b):
    return lax.dot_general(a, b, (((1,), (0,)), ((), ())), preferred_element_type=jnp.float32)


def push(src, dst, send, recv, device):
    pltpu.make_async_remote_copy(
        src_ref=src, dst_ref=dst, send_sem=send, recv_sem=recv, device_id=device, device_id_type=MESH
    ).start()


def keep(src, dst, sem):
    pltpu.make_async_copy(src, dst, sem).start()


def arrived(ref, sem):
    pltpu.make_async_copy(ref, ref, sem).wait()


def columns(head):
    return pl.ds(pl.multiple_of(head * DH, DH), DH)


def rows_of(start, count):
    return pl.ds(pl.multiple_of(start, 16), count)


def side_of(z):
    return lax.rem(lax.div(z + 1, 2), 2)


def block_at(y, which, side):
    x, later = lax.div(which, 2), lax.rem(which, 2)
    return (x * 2 + y) * 4 + side + later * (3 - 2 * side)


def head_at(section, seq):
    return lax.div(seq, 4) * 4 + lax.div(section, 2) * 2 + lax.div(lax.rem(seq, 4), 2)


def group_at(section, seq):
    return lax.rem(seq, 2) * 2 + lax.rem(section, 2)


def fill_bias(offs, first, bias):
    sub = lax.broadcasted_iota(jnp.int32, (RB, 1), 0)
    wide = 512

    def tile_bias(t, _):
        def some(j, _):
            flat = lax.broadcasted_iota(jnp.int32, (1, wide), 1) + j * wide
            half, side = lax.div(flat, KHALF), lax.rem(lax.div(flat, SIDE), 2)
            inside = lax.rem(flat, SIDE)
            which = lax.div(inside, HALF)
            block = block_at(lax.div(which, 8), lax.rem(which, 8), side)
            spot = block * (2 * HALF) + half * HALF + lax.rem(inside, HALF)
            cols = pl.ds(pl.multiple_of(j * wide, wide), wide)
            for k in range(GRP):
                qpos = sub + (first + offs[t * GRP + k])
                bias[t, k * RB : (k + 1) * RB, cols] = jnp.where(spot <= qpos, 0.0, -1e30)
            return 0

        lax.fori_loop(0, KLEN // wide, some, 0)
        return 0

    lax.fori_loop(0, TILES, tile_bias, 0)


def at_step(step, turn):
    return SECT - 1 - lax.div(step, TILES), lax.rem(step + turn, TILES)


def load_query(q_in, gains, step, turn):
    layer, t = at_step(step, turn)
    q = q_in[pl.ds(layer * SEQ + t * GRP, GRP)].reshape(TILE, DH)
    return (q.astype(jnp.float32) * gains[layer][0:1, :]).astype(jnp.bfloat16)


def split_query(q):
    scaled = q.astype(jnp.float32) * (SCALE * LOG2E)
    high = scaled.astype(jnp.bfloat16)
    low = (scaled - high.astype(jnp.float32)).astype(jnp.bfloat16)
    return jnp.concatenate([high, low], axis=1)


def scores(t, slot, kk, q2_s, bias, sc):
    s = fdot(q2_s[...], kk[...]) + bias[t]
    sc[slot] = s
    peak = jnp.full((TILE, DH), NO_PEAK, jnp.float32)
    for c in range(KLEN // DH):
        peak = jnp.maximum(peak, s[:, c * DH : (c + 1) * DH])
    return peak


def one_step(step, turn, peak, q_in, gains, k_in, grad, kk, vt, bias, sc, ex, dp, dkv, q2_s, up_s):
    layer, t = at_step(step, turn)
    after = jnp.minimum(step + 1, STEPS - 1)
    slot = lax.rem(step, 2)
    up_now = up_s[pl.ds(t * GRP, GRP)].reshape(TILE, DH)
    q2_s[...] = split_query(load_query(q_in, gains, after, turn))
    norm = jnp.zeros((TILE, DH), jnp.float32)
    delta = jnp.zeros((TILE, DH), jnp.float32)
    d = fdot(up_now, vt[...])
    e = jnp.exp2(sc[slot] - peak)
    dp[...] = d
    ex[...] = e.astype(jnp.bfloat16)
    ed = e * d
    for c in range(KLEN // DH):
        norm = norm + e[:, c * DH : (c + 1) * DH]
        delta = delta + ed[:, c * DH : (c + 1) * DH]
    peak_after = scores(at_step(after, turn)[1], 1 - slot, kk, q2_s, bias, sc)
    inv = 1.0 / jnp.sum(norm, axis=1, keepdims=True)
    delta = jnp.sum(delta, axis=1, keepdims=True) * inv
    q = load_query(q_in, gains, step, turn)
    qn = (q.astype(jnp.float32) * (inv * SCALE)).T.astype(jnp.bfloat16)
    un = (up_now.astype(jnp.float32) * inv).T.astype(jnp.bfloat16)
    e = ex[...]
    ds = e * (dp[...] - delta).astype(jnp.bfloat16)
    dq = fdot(ds, k_in[...])
    dkv[0] += fdot(qn, ds)
    dkv[1] += fdot(un, e)
    up = (up_now.astype(jnp.float32) + gains[layer][0:1, :] * (dq * (inv * SCALE))).astype(jnp.bfloat16)
    up = up.reshape(GRP, RB, DH)
    up_s[pl.ds(t * GRP, GRP)] = up
    grad[pl.ds(layer * SEQ + t * GRP, GRP)] = up
    return jnp.max(peak_after, axis=1, keepdims=True)


def fused_kernel(
    offs, acts, top, keys, vals, gains, acts_out, k_out, v_out,
    q_in, up_s, k_in, v_in, g_in, grad, kk, vt, bias, sc, ex, dp, dkv, q2_s,
    outgoing, from_core, part, from_chip, total, gain, send, recv, ready,
):
    section, seq = lax.axis_index("section"), lax.axis_index("seq")
    core, chip = lax.rem(section, 2), lax.div(section, 2)
    sibling = section + 1 - 2 * core
    across = section + 2 - 4 * chip
    me = section * SEQ + seq
    head, group = head_at(section, seq), group_at(section, seq)
    partner = seq + 1 - 2 * lax.rem(seq, 2)
    x, y, z = lax.div(seq, 8), lax.rem(lax.div(seq, 4), 2), lax.rem(seq, 4)
    side = side_of(z)
    turn = lax.rem(x + z, TILES)
    mine = rows_of(group * RB, RB)

    barrier = pltpu.get_barrier_semaphore()

    def hello(i, _):
        pl.semaphore_signal(barrier, inc=1, device_id=(section, lax.rem(seq + i, SEQ)), device_id_type=MESH)
        return 0

    lax.fori_loop(1, SEQ, hello, 0)
    for j in range(1, SECT):
        pl.semaphore_signal(barrier, inc=1, device_id=(lax.rem(section + j, SECT), seq), device_id_type=MESH)
    for up in range(2):
        gain[up] = jnp.broadcast_to(gains[:, columns(head_at(2 * up, seq))], (8, DH))
    fill_bias(offs, group * RB, bias)
    dkv[...] = jnp.zeros_like(dkv)
    pl.semaphore_wait(barrier, SEQ + SECT - 2)
    for j in range(1, SECT):
        pl.semaphore_signal(ready, inc=1, device_id=(lax.rem(section + j, SECT), seq), device_id_type=MESH)

    here = rows_of(core * KHALF + side * SIDE + (y * 8 + x * 2 + lax.div(z, 2)) * HALF, HALF)
    k_here, v_here = k_in.at[here], v_in.at[here]

    def send_cached(i, _):
        to = lax.rem(seq + i, SEQ)
        there = head_at(section, to)
        push(keys.at[core, :, columns(there)], k_here, send.at[0], recv.at[0], (section, to))
        push(vals.at[core, :, columns(there)], v_here, send.at[1], recv.at[1], (section, to))
        return 0

    def query_rows(to_section, to):
        return acts.at[rows_of(group_at(to_section, to) * RB, RB), columns(head_at(to_section, to))]

    def send_query(to_section, to):
        push(query_rows(to_section, to), q_in.at[me], send.at[3], recv.at[3 + section], (to_section, to))

    def send_queries():
        for j in range(1, SECT):
            send_query(lax.rem(section + j, SECT), seq)

        def some(i, _):
            for j in range(SECT):
                send_query(lax.rem(section + j, SECT), lax.rem(seq + i, SEQ))
            return 0

        lax.fori_loop(1, SEQ, some, 0)

    def top_rows(to):
        return top.at[rows_of(group_at(section, to) * RB, RB), columns(head_at(section, to))]

    def send_top(i, _):
        to = lax.rem(seq + i, SEQ)
        push(top_rows(to), up_s.at[seq], send.at[2], recv.at[2], (section, to))
        return 0

    keep(keys.at[core, :, columns(head)], k_here, recv.at[0])
    keep(vals.at[core, :, columns(head)], v_here, recv.at[1])
    keep(top_rows(seq), up_s.at[seq], recv.at[2])
    keep(query_rows(section, seq), q_in.at[me], recv.at[3 + section])
    keep(gain.at[chip], g_in.at[section], recv.at[7])

    lax.fori_loop(1, SEQ, send_cached, 0)
    pl.semaphore_wait(ready, SECT - 1)
    @pl.when(section == SECT - 1)
    def _():
        send_queries()

    for j in range(1, SECT):
        to_section = lax.rem(section + j, SECT)
        push(gain.at[lax.div(to_section, 2)], g_in.at[section], send.at[4], recv.at[7], (to_section, seq))
    lax.fori_loop(1, SEQ, send_top, 0)
    k_half, v_half = k_in.at[rows_of(core * KHALF, KHALF)], v_in.at[rows_of(core * KHALF, KHALF)]
    k_other, v_other = k_in.at[rows_of((1 - core) * KHALF, KHALF)], v_in.at[rows_of((1 - core) * KHALF, KHALF)]
    arrived(k_half, recv.at[0])
    push(k_half, k_half, send.at[5], recv.at[8], (sibling, seq))

    arrived(k_other, recv.at[8])
    kt = k_in[...].T
    kk[:DH, :] = kt
    kk[DH:, :] = kt
    arrived(v_half, recv.at[1])
    push(v_half, v_half, send.at[6], recv.at[9], (sibling, seq))
    arrived(v_other, recv.at[9])
    vt[...] = v_in[...].T
    @pl.when(section != SECT - 1)
    def _():
        send_queries()

    arrived(g_in, recv.at[7])
    arrived(q_in.at[pl.ds((SECT - 1) * SEQ, SEQ)], recv.at[3 + SECT - 1])
    q2_s[...] = split_query(load_query(q_in, g_in, 0, turn))
    peak = jnp.max(scores(turn, 0, kk, q2_s, bias, sc), axis=1, keepdims=True)
    arrived(up_s, recv.at[2])

    def send_grads(step):
        layer, t = at_step(step, turn)
        first = layer * SEQ + t * GRP

        def send_one(inside):
            push(
                grad.at[first + inside], acts_out.at[mine, columns(head)],
                send.at[7], recv.at[10], (layer, t * GRP + inside),
            )

        for k in range(1, GRP):
            send_one(lax.rem(seq + k, GRP))
        inside = lax.rem(seq, GRP)
        own = (layer == section) & (t == lax.div(seq, GRP))

        @pl.when(own)
        def _():
            keep(grad.at[first + inside], acts_out.at[mine, columns(head)], recv.at[10])

        @pl.when(jnp.logical_not(own))
        def _():
            send_one(inside)

    def attend(step, peak):
        layer = SECT - 1 - lax.div(step, TILES)

        @pl.when((lax.rem(step, TILES) == TILES - 1) & (layer > 0))
        def _():
            arrived(q_in.at[pl.ds((layer - 1) * SEQ, SEQ)], recv.at[2 + layer])

        return one_step(step, turn, peak, q_in, g_in, k_in, grad, kk, vt, bias, sc, ex, dp, dkv, q2_s, up_s)

    def attend_send(step, peak):
        peak = attend(step, peak)
        send_grads(step)
        return peak

    lax.fori_loop(0, STEPS, attend_send, peak)

    near_half = pl.ds(pl.multiple_of(core * KHALF, DH), KHALF)
    far_half = pl.ds(pl.multiple_of((1 - core) * KHALF, DH), KHALF)
    for kv in range(2):
        outgoing[kv] = dkv[kv, :, far_half].astype(jnp.bfloat16).T
        push(outgoing.at[kv], from_core.at[kv], send.at[8 + kv], recv.at[11 + kv], (sibling, seq))

    def add_core(kv, rows):
        return part[kv, rows].astype(jnp.float32) + from_core[kv, rows].astype(jnp.float32)

    def piece(p):
        return lax.rem(y + p, 2) * PROWS

    for kv in range(2):
        part[kv] = dkv[kv, :, near_half].astype(jnp.bfloat16).T
        arrived(from_core.at[kv], recv.at[11 + kv])
        for p in range(2):
            rows = rows_of((1 - side) * SIDE + piece(p), PROWS)
            part[kv, rows] = add_core(kv, rows).astype(jnp.bfloat16)
            push(
                part.at[kv, rows], from_chip.at[kv, rows_of(piece(p), PROWS)],
                send.at[10], recv.at[13 + 2 * kv + p], (section, partner),
            )

    def send_totals(kv, p, target):
        def some(i, _):
            which = lax.rem(2 * (x + z) + section + i, PBLOCKS)
            block = block_at(lax.rem(y + p, 2), which, side)
            src = total.at[kv, rows_of(piece(p) + which * HALF, HALF)]

            @pl.when(block == seq)
            def _():
                keep(src, target, recv.at[17 + kv])

            @pl.when(block != seq)
            def _():
                push(src, target, send.at[11 + kv], recv.at[17 + kv], (section, block))

            push(src, target, send.at[11 + kv], recv.at[17 + kv], (across, block))
            return 0

        lax.fori_loop(0, PBLOCKS, some, 0)

    for kv, out in ((0, k_out), (1, v_out)):
        for p in range(2):
            done = rows_of(piece(p), PROWS)
            arrived(from_chip.at[kv, done], recv.at[13 + 2 * kv + p])
            total[kv, done] = (
                add_core(kv, rows_of(side * SIDE + piece(p), PROWS)) + from_chip[kv, done].astype(jnp.float32)
            ).astype(jnp.bfloat16)
            send_totals(kv, p, out.at[core, :, columns(head)])

    for kv, out in ((0, k_out), (1, v_out)):
        arrived(out.at[core], recv.at[17 + kv])
        push(out.at[core], out.at[core], send.at[13 + kv], recv.at[19 + kv], (sibling, seq))
    arrived(acts_out, recv.at[10])
    for kv, out in ((0, k_out), (1, v_out)):
        arrived(out.at[1 - core], recv.at[19 + kv])

    arrived(k_in.at[: (SEQ - 1) * HALF], send.at[0])
    arrived(v_in.at[: (SEQ - 1) * HALF], send.at[1])
    arrived(up_s.at[: SEQ - 1], send.at[2])
    arrived(q_in.at[: ALL - 1], send.at[3])
    arrived(g_in.at[: SECT - 1], send.at[4])
    arrived(k_half, send.at[5])
    arrived(v_half, send.at[6])
    arrived(grad.at[: ALL - 1], send.at[7])
    arrived(from_chip, send.at[10])
    for kv, out in ((0, k_out), (1, v_out)):
        arrived(outgoing.at[kv], send.at[8 + kv])
        arrived(k_in.at[: (SEQ - 1) * HALF], send.at[11 + kv])
        arrived(out.at[core], send.at[13 + kv])


def attention_grads(offs, acts, top, keys, vals, gains):
    bf = jnp.bfloat16
    any_space = pl.BlockSpec(memory_space=pl.ANY)
    return pl.pallas_call(
        fused_kernel,
        out_shape=(
            jax.ShapeDtypeStruct((SECT * RB, SEQ * DH), bf),
            jax.ShapeDtypeStruct((2, HALF, SEQ * DH), bf),
            jax.ShapeDtypeStruct((2, HALF, SEQ * DH), bf),
        ),
        in_specs=[pl.BlockSpec(memory_space=pltpu.SMEM)] + [any_space] * 4 + [pl.BlockSpec(memory_space=pltpu.VMEM)],
        out_specs=(any_space, any_space, any_space),
        scratch_shapes=[
            pltpu.VMEM((ALL, RB, DH), bf),
            pltpu.VMEM((SEQ, RB, DH), bf),
            pltpu.VMEM((KLEN, DH), bf),
            pltpu.VMEM((KLEN, DH), bf),
            pltpu.VMEM((SECT, 8, DH), jnp.float32),
            pltpu.VMEM((ALL, RB, DH), bf),
            pltpu.VMEM((2 * DH, KLEN), bf),
            pltpu.VMEM((DH, KLEN), bf),
            pltpu.VMEM((TILES, TILE, KLEN), jnp.float32),
            pltpu.VMEM((2, TILE, KLEN), jnp.float32),
            pltpu.VMEM((TILE, KLEN), bf),
            pltpu.VMEM((TILE, KLEN), jnp.float32),
            pltpu.VMEM((2, DH, KLEN), jnp.float32),
            pltpu.VMEM((TILE, 2 * DH), bf),
            pltpu.VMEM((2, KHALF, DH), bf),
            pltpu.VMEM((2, KHALF, DH), bf),
            pltpu.VMEM((2, KHALF, DH), bf),
            pltpu.VMEM((2, SIDE, DH), bf),
            pltpu.VMEM((2, SIDE, DH), bf),
            pltpu.VMEM((2, 8, DH), jnp.float32),
            pltpu.SemaphoreType.DMA((15,)),
            pltpu.SemaphoreType.DMA((21,)),
            pltpu.SemaphoreType.REGULAR,
        ],
        compiler_params=pltpu.CompilerParams(
            collective_id=0, has_side_effects=True, vmem_limit_bytes=60 * 2**20
        ),
    )(offs, acts, top, keys, vals, gains)


def store_kernel(a, b, c, a_out, b_out, c_out, sems):
    copies = [
        pltpu.make_async_copy(src, dst, sems.at[i])
        for i, (src, dst) in enumerate(((a, a_out), (b, b_out), (c, c_out)))
    ]
    for copy in copies:
        copy.start()
    for copy in copies:
        copy.wait()


def store(*arrays):
    any_space = pl.BlockSpec(memory_space=pl.ANY)
    return pl.pallas_call(
        store_kernel,
        out_shape=tuple(jax.ShapeDtypeStruct(a.shape, a.dtype) for a in arrays),
        in_specs=[pl.BlockSpec(memory_space=pltpu.VMEM)] * 3,
        out_specs=(any_space,) * 3,
        scratch_shapes=[pltpu.SemaphoreType.DMA((3,))],
    )(*arrays)


def local(acts, gains, grad_top, keys, values, offsets):
    out_acts, out_keys, out_values = attention_grads(
        offsets, acts[0], grad_top, keys.reshape(2, HALF, -1), values.reshape(2, HALF, -1), gains
    )
    out_acts, out_keys, out_values = store(out_acts, out_keys, out_values)
    return (out_acts[None], out_keys.reshape(2 * HALF, -1), out_values.reshape(2 * HALF, -1))


def solution(mesh):
    return jax.shard_map(
        local,
        mesh=mesh,
        in_specs=(
            P("section", "seq", None),
            P("section", None),
            P("seq", None),
            P("seq", None),
            P("seq", None),
            P(),
        ),
        out_specs=(P("section", "seq", None), P("seq", None), P("seq", None)),
        check_vma=False,
    )
```

```python
import jax
import jax.numpy as jnp
from jax import lax
from jax.experimental import pallas as pl
from jax.experimental.pallas import tpu as pltpu
from jax.sharding import PartitionSpec as P

DH = 128
SECT = 4
SEQ = 32
ALL = SECT * SEQ
RB = 32
HALF = 48
KHALF = SEQ * HALF
KLEN = 2 * KHALF
TILE = 256
GRP = TILE // RB
TILES = SEQ // GRP
STEPS = SECT * TILES
SIDE = KHALF // 2
PBLOCKS = 8
PROWS = PBLOCKS * HALF
SCALE = 1.0 / DH**0.5
LOG2E = 1.4426950408889634
NO_PEAK = -3e38
MESH = pl.DeviceIdType.MESH


def fdot(a, b):
    return lax.dot_general(a, b, (((1,), (0,)), ((), ())), preferred_element_type=jnp.float32)


def push(src, dst, send, recv, device):
    pltpu.make_async_remote_copy(
        src_ref=src, dst_ref=dst, send_sem=send, recv_sem=recv, device_id=device, device_id_type=MESH
    ).start()


def keep(src, dst, sem):
    pltpu.make_async_copy(src, dst, sem).start()


def arrived(ref, sem):
    pltpu.make_async_copy(ref, ref, sem).wait()


def columns(head):
    return pl.ds(pl.multiple_of(head * DH, DH), DH)


def rows_of(start, count):
    return pl.ds(pl.multiple_of(start, 16), count)


def side_of(z):
    return lax.rem(lax.div(z + 1, 2), 2)


def block_at(y, which, side):
    x, later = lax.div(which, 2), lax.rem(which, 2)
    return (x * 2 + y) * 4 + side + later * (3 - 2 * side)


def head_at(section, seq):
    return lax.div(seq, 4) * 4 + lax.div(section, 2) * 2 + lax.div(lax.rem(seq, 4), 2)


def group_at(section, seq):
    return lax.rem(seq, 2) * 2 + lax.rem(section, 2)


def fill_bias(offs, first, bias):
    sub = lax.broadcasted_iota(jnp.int32, (RB, 1), 0)
    wide = 512

    def tile_bias(t, _):
        def some(j, _):
            flat = lax.broadcasted_iota(jnp.int32, (1, wide), 1) + j * wide
            half, side = lax.div(flat, KHALF), lax.rem(lax.div(flat, SIDE), 2)
            inside = lax.rem(flat, SIDE)
            which = lax.div(inside, HALF)
            block = block_at(lax.div(which, 8), lax.rem(which, 8), side)
            spot = block * (2 * HALF) + half * HALF + lax.rem(inside, HALF)
            cols = pl.ds(pl.multiple_of(j * wide, wide), wide)
            for k in range(GRP):
                qpos = sub + (first + offs[t * GRP + k])
                bias[t, k * RB : (k + 1) * RB, cols] = jnp.where(spot <= qpos, 0.0, -1e30)
            return 0

        lax.fori_loop(0, KLEN // wide, some, 0)
        return 0

    lax.fori_loop(0, TILES, tile_bias, 0)


def at_step(step, turn):
    return SECT - 1 - lax.div(step, TILES), lax.rem(step + turn, TILES)


def load_query(q_in, gains, step, turn):
    layer, t = at_step(step, turn)
    q = q_in[pl.ds(layer * SEQ + t * GRP, GRP)].reshape(TILE, DH)
    return (q.astype(jnp.float32) * gains[layer][0:1, :]).astype(jnp.bfloat16)


def split_query(q):
    scaled = q.astype(jnp.float32) * (SCALE * LOG2E)
    high = scaled.astype(jnp.bfloat16)
    low = (scaled - high.astype(jnp.float32)).astype(jnp.bfloat16)
    return jnp.concatenate([high, low], axis=1)


def scores(t, slot, kk, q2_s, bias, sc):
    s = fdot(q2_s[...], kk[...]) + bias[t]
    sc[slot] = s
    peak = jnp.full((TILE, DH), NO_PEAK, jnp.float32)
    for c in range(KLEN // DH):
        peak = jnp.maximum(peak, s[:, c * DH : (c + 1) * DH])
    return peak


def one_step(step, turn, peak, q_in, gains, k_in, grad, kk, vt, bias, sc, ex, dp, dkv, q2_s, up_s):
    layer, t = at_step(step, turn)
    after = jnp.minimum(step + 1, STEPS - 1)
    slot = lax.rem(step, 2)
    up_now = up_s[pl.ds(t * GRP, GRP)].reshape(TILE, DH)
    q2_s[...] = split_query(load_query(q_in, gains, after, turn))
    norm = jnp.zeros((TILE, DH), jnp.float32)
    delta = jnp.zeros((TILE, DH), jnp.float32)
    d = fdot(up_now, vt[...])
    e = jnp.exp2(sc[slot] - peak)
    dp[...] = d
    ex[...] = e.astype(jnp.bfloat16)
    ed = e * d
    for c in range(KLEN // DH):
        norm = norm + e[:, c * DH : (c + 1) * DH]
        delta = delta + ed[:, c * DH : (c + 1) * DH]
    peak_after = scores(at_step(after, turn)[1], 1 - slot, kk, q2_s, bias, sc)
    inv = 1.0 / jnp.sum(norm, axis=1, keepdims=True)
    delta = jnp.sum(delta, axis=1, keepdims=True) * inv
    q = load_query(q_in, gains, step, turn)
    qn = (q.astype(jnp.float32) * (inv * SCALE)).T.astype(jnp.bfloat16)
    un = (up_now.astype(jnp.float32) * inv).T.astype(jnp.bfloat16)
    e = ex[...]
    ds = e * (dp[...] - delta).astype(jnp.bfloat16)
    dq = fdot(ds, k_in[...])
    dkv[0] += fdot(qn, ds)
    dkv[1] += fdot(un, e)
    up = (up_now.astype(jnp.float32) + gains[layer][0:1, :] * (dq * (inv * SCALE))).astype(jnp.bfloat16)
    up = up.reshape(GRP, RB, DH)
    up_s[pl.ds(t * GRP, GRP)] = up
    grad[pl.ds(layer * SEQ + t * GRP, GRP)] = up
    return jnp.max(peak_after, axis=1, keepdims=True)


def fused_kernel(
    offs, acts, top, keys, vals, gains, acts_out, k_out, v_out,
    q_in, up_s, k_in, v_in, g_in, grad, kk, vt, bias, sc, ex, dp, dkv, q2_s,
    outgoing, from_core, part, from_chip, total, gain, send, recv, ready,
):
    section, seq = lax.axis_index("section"), lax.axis_index("seq")
    core, chip = lax.rem(section, 2), lax.div(section, 2)
    sibling = section + 1 - 2 * core
    across = section + 2 - 4 * chip
    me = section * SEQ + seq
    head, group = head_at(section, seq), group_at(section, seq)
    partner = seq + 1 - 2 * lax.rem(seq, 2)
    x, y, z = lax.div(seq, 8), lax.rem(lax.div(seq, 4), 2), lax.rem(seq, 4)
    side = side_of(z)
    turn = lax.rem(x + z, TILES)
    mine = rows_of(group * RB, RB)

    barrier = pltpu.get_barrier_semaphore()

    def hello(i, _):
        pl.semaphore_signal(barrier, inc=1, device_id=(section, lax.rem(seq + i, SEQ)), device_id_type=MESH)
        return 0

    lax.fori_loop(1, SEQ, hello, 0)
    for j in range(1, SECT):
        pl.semaphore_signal(barrier, inc=1, device_id=(lax.rem(section + j, SECT), seq), device_id_type=MESH)
    for up in range(2):
        gain[up] = jnp.broadcast_to(gains[:, columns(head_at(2 * up, seq))], (8, DH))
    fill_bias(offs, group * RB, bias)
    dkv[...] = jnp.zeros_like(dkv)
    pl.semaphore_wait(barrier, SEQ + SECT - 2)
    for j in range(1, SECT):
        pl.semaphore_signal(ready, inc=1, device_id=(lax.rem(section + j, SECT), seq), device_id_type=MESH)

    here = rows_of(core * KHALF + side * SIDE + (y * 8 + x * 2 + lax.div(z, 2)) * HALF, HALF)
    k_here, v_here = k_in.at[here], v_in.at[here]

    def send_cached(i, _):
        to = lax.rem(seq + i, SEQ)
        there = head_at(section, to)
        push(keys.at[core, :, columns(there)], k_here, send.at[0], recv.at[0], (section, to))
        push(vals.at[core, :, columns(there)], v_here, send.at[1], recv.at[1], (section, to))
        return 0

    def query_rows(to_section, to):
        return acts.at[rows_of(group_at(to_section, to) * RB, RB), columns(head_at(to_section, to))]

    def send_query(to_section, to):
        push(query_rows(to_section, to), q_in.at[me], send.at[3], recv.at[3 + section], (to_section, to))

    def send_queries():
        for j in range(1, SECT):
            send_query(lax.rem(section + j, SECT), seq)

        def some(i, _):
            for j in range(SECT):
                send_query(lax.rem(section + j, SECT), lax.rem(seq + i, SEQ))
            return 0

        lax.fori_loop(1, SEQ, some, 0)

    def top_rows(to):
        return top.at[rows_of(group_at(section, to) * RB, RB), columns(head_at(section, to))]

    def send_top(i, _):
        to = lax.rem(seq + i, SEQ)
        push(top_rows(to), up_s.at[seq], send.at[2], recv.at[2], (section, to))
        return 0

    keep(keys.at[core, :, columns(head)], k_here, recv.at[0])
    keep(vals.at[core, :, columns(head)], v_here, recv.at[1])
    keep(top_rows(seq), up_s.at[seq], recv.at[2])
    keep(query_rows(section, seq), q_in.at[me], recv.at[3 + section])
    keep(gain.at[chip], g_in.at[section], recv.at[7])

    lax.fori_loop(1, SEQ, send_cached, 0)
    pl.semaphore_wait(ready, SECT - 1)
    @pl.when(section == SECT - 1)
    def _():
        send_queries()

    for j in range(1, SECT):
        to_section = lax.rem(section + j, SECT)
        push(gain.at[lax.div(to_section, 2)], g_in.at[section], send.at[4], recv.at[7], (to_section, seq))
    lax.fori_loop(1, SEQ, send_top, 0)
    k_half, v_half = k_in.at[rows_of(core * KHALF, KHALF)], v_in.at[rows_of(core * KHALF, KHALF)]
    k_other, v_other = k_in.at[rows_of((1 - core) * KHALF, KHALF)], v_in.at[rows_of((1 - core) * KHALF, KHALF)]
    arrived(k_half, recv.at[0])
    push(k_half, k_half, send.at[5], recv.at[8], (sibling, seq))

    arrived(k_other, recv.at[8])
    kt = k_in[...].T
    kk[:DH, :] = kt
    kk[DH:, :] = kt
    arrived(v_half, recv.at[1])
    push(v_half, v_half, send.at[6], recv.at[9], (sibling, seq))
    arrived(v_other, recv.at[9])
    vt[...] = v_in[...].T
    @pl.when(section != SECT - 1)
    def _():
        send_queries()

    arrived(g_in, recv.at[7])
    arrived(q_in.at[pl.ds((SECT - 1) * SEQ, SEQ)], recv.at[3 + SECT - 1])
    q2_s[...] = split_query(load_query(q_in, g_in, 0, turn))
    peak = jnp.max(scores(turn, 0, kk, q2_s, bias, sc), axis=1, keepdims=True)
    arrived(up_s, recv.at[2])

    def send_grads(step):
        layer, t = at_step(step, turn)
        first = layer * SEQ + t * GRP

        def send_one(inside):
            push(
                grad.at[first + inside], acts_out.at[mine, columns(head)],
                send.at[7], recv.at[10], (layer, t * GRP + inside),
            )

        for k in range(1, GRP):
            send_one(lax.rem(seq + k, GRP))
        inside = lax.rem(seq, GRP)
        own = (layer == section) & (t == lax.div(seq, GRP))

        @pl.when(own)
        def _():
            keep(grad.at[first + inside], acts_out.at[mine, columns(head)], recv.at[10])

        @pl.when(jnp.logical_not(own))
        def _():
            send_one(inside)

    def attend(step, peak):
        layer = SECT - 1 - lax.div(step, TILES)

        @pl.when((lax.rem(step, TILES) == TILES - 1) & (layer > 0))
        def _():
            arrived(q_in.at[pl.ds((layer - 1) * SEQ, SEQ)], recv.at[2 + layer])

        return one_step(step, turn, peak, q_in, g_in, k_in, grad, kk, vt, bias, sc, ex, dp, dkv, q2_s, up_s)

    def attend_send(step, peak):
        peak = attend(step, peak)
        send_grads(step)
        return peak

    lax.fori_loop(0, STEPS, attend_send, peak)

    near_half = pl.ds(pl.multiple_of(core * KHALF, DH), KHALF)
    far_half = pl.ds(pl.multiple_of((1 - core) * KHALF, DH), KHALF)
    for kv in range(2):
        outgoing[kv] = dkv[kv, :, far_half].astype(jnp.bfloat16).T
        push(outgoing.at[kv], from_core.at[kv], send.at[8 + kv], recv.at[11 + kv], (sibling, seq))

    def add_core(kv, rows):
        return part[kv, rows].astype(jnp.float32) + from_core[kv, rows].astype(jnp.float32)

    def piece(p):
        return lax.rem(y + p, 2) * PROWS

    for kv in range(2):
        part[kv] = dkv[kv, :, near_half].astype(jnp.bfloat16).T
        arrived(from_core.at[kv], recv.at[11 + kv])
        for p in range(2):
            rows = rows_of((1 - side) * SIDE + piece(p), PROWS)
            part[kv, rows] = add_core(kv, rows).astype(jnp.bfloat16)
            push(
                part.at[kv, rows], from_chip.at[kv, rows_of(piece(p), PROWS)],
                send.at[10], recv.at[13 + 2 * kv + p], (section, partner),
            )

    def send_totals(kv, p, target):
        def some(i, _):
            which = lax.rem(2 * (x + z) + section + i, PBLOCKS)
            block = block_at(lax.rem(y + p, 2), which, side)
            src = total.at[kv, rows_of(piece(p) + which * HALF, HALF)]

            @pl.when(block == seq)
            def _():
                keep(src, target, recv.at[17 + kv])

            @pl.when(block != seq)
            def _():
                push(src, target, send.at[11 + kv], recv.at[17 + kv], (section, block))

            push(src, target, send.at[11 + kv], recv.at[17 + kv], (across, block))
            return 0

        lax.fori_loop(0, PBLOCKS, some, 0)

    for kv, out in ((0, k_out), (1, v_out)):
        for p in range(2):
            done = rows_of(piece(p), PROWS)
            arrived(from_chip.at[kv, done], recv.at[13 + 2 * kv + p])
            total[kv, done] = (
                add_core(kv, rows_of(side * SIDE + piece(p), PROWS)) + from_chip[kv, done].astype(jnp.float32)
            ).astype(jnp.bfloat16)
            send_totals(kv, p, out.at[core, :, columns(head)])

    for kv, out in ((0, k_out), (1, v_out)):
        arrived(out.at[core], recv.at[17 + kv])
        push(out.at[core], out.at[core], send.at[13 + kv], recv.at[19 + kv], (sibling, seq))
    arrived(acts_out, recv.at[10])
    for kv, out in ((0, k_out), (1, v_out)):
        arrived(out.at[1 - core], recv.at[19 + kv])

    arrived(k_in.at[: (SEQ - 1) * HALF], send.at[0])
    arrived(v_in.at[: (SEQ - 1) * HALF], send.at[1])
    arrived(up_s.at[: SEQ - 1], send.at[2])
    arrived(q_in.at[: ALL - 1], send.at[3])
    arrived(g_in.at[: SECT - 1], send.at[4])
    arrived(k_half, send.at[5])
    arrived(v_half, send.at[6])
    arrived(grad.at[: ALL - 1], send.at[7])
    arrived(from_chip, send.at[10])
    for kv, out in ((0, k_out), (1, v_out)):
        arrived(outgoing.at[kv], send.at[8 + kv])
        arrived(k_in.at[: (SEQ - 1) * HALF], send.at[11 + kv])
        arrived(out.at[core], send.at[13 + kv])


def attention_grads(offs, acts, top, keys, vals, gains):
    bf = jnp.bfloat16
    any_space = pl.BlockSpec(memory_space=pl.ANY)
    return pl.pallas_call(
        fused_kernel,
        out_shape=(
            jax.ShapeDtypeStruct((SECT * RB, SEQ * DH), bf),
            jax.ShapeDtypeStruct((2, HALF, SEQ * DH), bf),
            jax.ShapeDtypeStruct((2, HALF, SEQ * DH), bf),
        ),
        in_specs=[pl.BlockSpec(memory_space=pltpu.SMEM)] + [any_space] * 4 + [pl.BlockSpec(memory_space=pltpu.VMEM)],
        out_specs=(any_space, any_space, any_space),
        scratch_shapes=[
            pltpu.VMEM((ALL, RB, DH), bf),
            pltpu.VMEM((SEQ, RB, DH), bf),
            pltpu.VMEM((KLEN, DH), bf),
            pltpu.VMEM((KLEN, DH), bf),
            pltpu.VMEM((SECT, 8, DH), jnp.float32),
            pltpu.VMEM((ALL, RB, DH), bf),
            pltpu.VMEM((2 * DH, KLEN), bf),
            pltpu.VMEM((DH, KLEN), bf),
            pltpu.VMEM((TILES, TILE, KLEN), jnp.float32),
            pltpu.VMEM((2, TILE, KLEN), jnp.float32),
            pltpu.VMEM((TILE, KLEN), bf),
            pltpu.VMEM((TILE, KLEN), jnp.float32),
            pltpu.VMEM((2, DH, KLEN), jnp.float32),
            pltpu.VMEM((TILE, 2 * DH), bf),
            pltpu.VMEM((2, KHALF, DH), bf),
            pltpu.VMEM((2, KHALF, DH), bf),
            pltpu.VMEM((2, KHALF, DH), bf),
            pltpu.VMEM((2, SIDE, DH), bf),
            pltpu.VMEM((2, SIDE, DH), bf),
            pltpu.VMEM((2, 8, DH), jnp.float32),
            pltpu.SemaphoreType.DMA((15,)),
            pltpu.SemaphoreType.DMA((21,)),
            pltpu.SemaphoreType.REGULAR,
        ],
        compiler_params=pltpu.CompilerParams(
            collective_id=0, has_side_effects=True, vmem_limit_bytes=60 * 2**20
        ),
    )(offs, acts, top, keys, vals, gains)


def store_kernel(a, b, c, a_out, b_out, c_out, a_tmp, b_tmp, c_tmp, sems):
    parts = []
    for src, tmp, dst in ((a, a_tmp, a_out), (b, b_tmp, b_out), (c, c_tmp, c_out)):
        half = src.shape[1] // 2
        for cols in (slice(0, half), slice(half, 2 * half)):
            n = len(parts)
            parts.append((
                pltpu.make_async_copy(src.at[:, cols], tmp.at[:, cols], sems.at[0, n]),
                pltpu.make_async_copy(tmp.at[:, cols], dst.at[:, cols], sems.at[1, n]),
            ))
    for load, _ in parts:
        load.start()
    for load, save in parts:
        load.wait()
        save.start()
    for _, save in parts:
        save.wait()


def store(*arrays):
    any_space = pl.BlockSpec(memory_space=pl.ANY)
    return pl.pallas_call(
        store_kernel,
        out_shape=tuple(jax.ShapeDtypeStruct(a.shape, a.dtype) for a in arrays),
        in_specs=[any_space] * 3,
        out_specs=(any_space,) * 3,
        scratch_shapes=[pltpu.VMEM(a.shape, a.dtype) for a in arrays] + [pltpu.SemaphoreType.DMA((2, 6))],
    )(*arrays)


def local(acts, gains, grad_top, keys, values, offsets):
    out_acts, out_keys, out_values = attention_grads(
        offsets, acts[0], grad_top, keys.reshape(2, HALF, -1), values.reshape(2, HALF, -1), gains
    )
    out_acts, out_keys, out_values = store(
        out_acts, out_keys.reshape(2 * HALF, -1), out_values.reshape(2 * HALF, -1)
    )
    return (out_acts[None], out_keys, out_values)


def solution(mesh):
    return jax.shard_map(
        local,
        mesh=mesh,
        in_specs=(
            P("section", "seq", None),
            P("section", None),
            P("seq", None),
            P("seq", None),
            P("seq", None),
            P(),
        ),
        out_specs=(P("section", "seq", None), P("seq", None), P("seq", None)),
        check_vma=False,
    )
```

```python
import jax
import jax.numpy as jnp
from jax import lax
from jax.experimental import pallas as pl
from jax.experimental.pallas import tpu as pltpu
from jax.sharding import PartitionSpec as P

DH = 128
SECT = 4
SEQ = 32
ALL = SECT * SEQ
RB = 32
HALF = 48
KHALF = SEQ * HALF
KLEN = 2 * KHALF
TILE = 256
GRP = TILE // RB
TILES = SEQ // GRP
STEPS = SECT * TILES
SIDE = KHALF // 2
PBLOCKS = 8
PROWS = PBLOCKS * HALF
SCALE = 1.0 / DH**0.5
LOG2E = 1.4426950408889634
NO_PEAK = -3e38
MESH = pl.DeviceIdType.MESH


def fdot(a, b):
    return lax.dot_general(a, b, (((1,), (0,)), ((), ())), preferred_element_type=jnp.float32)


def push(src, dst, send, recv, device):
    pltpu.make_async_remote_copy(
        src_ref=src, dst_ref=dst, send_sem=send, recv_sem=recv, device_id=device, device_id_type=MESH
    ).start()


def keep(src, dst, sem):
    pltpu.make_async_copy(src, dst, sem).start()


def arrived(ref, sem):
    pltpu.make_async_copy(ref, ref, sem).wait()


def columns(head):
    return pl.ds(pl.multiple_of(head * DH, DH), DH)


def rows_of(start, count):
    return pl.ds(pl.multiple_of(start, 16), count)


def side_of(z):
    return lax.rem(lax.div(z + 1, 2), 2)


def block_at(y, which, side):
    x, later = lax.div(which, 2), lax.rem(which, 2)
    return (x * 2 + y) * 4 + side + later * (3 - 2 * side)


def head_at(section, seq):
    return lax.div(seq, 4) * 4 + lax.div(section, 2) * 2 + lax.div(lax.rem(seq, 4), 2)


def group_at(section, seq):
    return lax.rem(seq, 2) * 2 + lax.rem(section, 2)


def fill_bias(offs, first, bias):
    sub = lax.broadcasted_iota(jnp.int32, (RB, 1), 0)
    wide = 512

    def tile_bias(t, _):
        def some(j, _):
            flat = lax.broadcasted_iota(jnp.int32, (1, wide), 1) + j * wide
            half, side = lax.div(flat, KHALF), lax.rem(lax.div(flat, SIDE), 2)
            inside = lax.rem(flat, SIDE)
            which = lax.div(inside, HALF)
            block = block_at(lax.div(which, 8), lax.rem(which, 8), side)
            spot = block * (2 * HALF) + half * HALF + lax.rem(inside, HALF)
            cols = pl.ds(pl.multiple_of(j * wide, wide), wide)
            for k in range(GRP):
                qpos = sub + (first + offs[t * GRP + k])
                bias[t, k * RB : (k + 1) * RB, cols] = jnp.where(spot <= qpos, 0.0, -1e30)
            return 0

        lax.fori_loop(0, KLEN // wide, some, 0)
        return 0

    lax.fori_loop(0, TILES, tile_bias, 0)


def at_step(step, turn):
    return SECT - 1 - lax.div(step, TILES), lax.rem(step + turn, TILES)


def load_query(q_in, gains, step, turn):
    layer, t = at_step(step, turn)
    q = q_in[pl.ds(layer * SEQ + t * GRP, GRP)].reshape(TILE, DH)
    return (q.astype(jnp.float32) * gains[layer][0:1, :]).astype(jnp.bfloat16)


def split_query(q):
    scaled = q.astype(jnp.float32) * (SCALE * LOG2E)
    high = scaled.astype(jnp.bfloat16)
    low = (scaled - high.astype(jnp.float32)).astype(jnp.bfloat16)
    return jnp.concatenate([high, low], axis=1)


def scores(t, slot, kk, q2_s, bias, sc):
    s = fdot(q2_s[...], kk[...]) + bias[t]
    sc[slot] = s
    peak = jnp.full((TILE, DH), NO_PEAK, jnp.float32)
    for c in range(KLEN // DH):
        peak = jnp.maximum(peak, s[:, c * DH : (c + 1) * DH])
    return peak


def one_step(step, turn, peak, q_in, gains, k_in, grad, kk, vt, bias, sc, ex, dp, dkv, q2_s, up_s):
    layer, t = at_step(step, turn)
    after = jnp.minimum(step + 1, STEPS - 1)
    slot = lax.rem(step, 2)
    up_now = up_s[pl.ds(t * GRP, GRP)].reshape(TILE, DH)
    q2_s[...] = split_query(load_query(q_in, gains, after, turn))
    norm = jnp.zeros((TILE, DH), jnp.float32)
    delta = jnp.zeros((TILE, DH), jnp.float32)
    d = fdot(up_now, vt[...])
    e = jnp.exp2(sc[slot] - peak)
    dp[...] = d
    ex[...] = e.astype(jnp.bfloat16)
    ed = e * d
    for c in range(KLEN // DH):
        norm = norm + e[:, c * DH : (c + 1) * DH]
        delta = delta + ed[:, c * DH : (c + 1) * DH]
    peak_after = scores(at_step(after, turn)[1], 1 - slot, kk, q2_s, bias, sc)
    inv = 1.0 / jnp.sum(norm, axis=1, keepdims=True)
    delta = jnp.sum(delta, axis=1, keepdims=True) * inv
    q = load_query(q_in, gains, step, turn)
    qn = (q.astype(jnp.float32) * (inv * SCALE)).T.astype(jnp.bfloat16)
    un = (up_now.astype(jnp.float32) * inv).T.astype(jnp.bfloat16)
    e = ex[...]
    ds = e * (dp[...] - delta).astype(jnp.bfloat16)
    dq = fdot(ds, k_in[...])
    dkv[0] += fdot(qn, ds)
    dkv[1] += fdot(un, e)
    up = (up_now.astype(jnp.float32) + gains[layer][0:1, :] * (dq * (inv * SCALE))).astype(jnp.bfloat16)
    up = up.reshape(GRP, RB, DH)
    up_s[pl.ds(t * GRP, GRP)] = up
    grad[pl.ds(layer * SEQ + t * GRP, GRP)] = up
    return jnp.max(peak_after, axis=1, keepdims=True)


def fused_kernel(
    offs, acts, top, keys, vals, gains, acts_out, k_out, v_out,
    q_in, up_s, k_in, v_in, g_in, grad, kk, vt, bias, sc, ex, dp, dkv, q2_s,
    outgoing, from_core, part, from_chip, total, gain, send, recv, ready,
):
    section, seq = lax.axis_index("section"), lax.axis_index("seq")
    core, chip = lax.rem(section, 2), lax.div(section, 2)
    sibling = section + 1 - 2 * core
    across = section + 2 - 4 * chip
    me = section * SEQ + seq
    head, group = head_at(section, seq), group_at(section, seq)
    partner = seq + 1 - 2 * lax.rem(seq, 2)
    x, y, z = lax.div(seq, 8), lax.rem(lax.div(seq, 4), 2), lax.rem(seq, 4)
    side = side_of(z)
    turn = lax.rem(x + z, TILES)
    mine = rows_of(group * RB, RB)

    barrier = pltpu.get_barrier_semaphore()

    def hello(i, _):
        pl.semaphore_signal(barrier, inc=1, device_id=(section, lax.rem(seq + i, SEQ)), device_id_type=MESH)
        return 0

    lax.fori_loop(1, SEQ, hello, 0)
    for j in range(1, SECT):
        pl.semaphore_signal(barrier, inc=1, device_id=(lax.rem(section + j, SECT), seq), device_id_type=MESH)
    for up in range(2):
        gain[up] = jnp.broadcast_to(gains[:, columns(head_at(2 * up, seq))], (8, DH))
    fill_bias(offs, group * RB, bias)
    dkv[...] = jnp.zeros_like(dkv)
    pl.semaphore_wait(barrier, SEQ + SECT - 2)
    for j in range(1, SECT):
        pl.semaphore_signal(ready, inc=1, device_id=(lax.rem(section + j, SECT), seq), device_id_type=MESH)

    here = rows_of(core * KHALF + side * SIDE + (y * 8 + x * 2 + lax.div(z, 2)) * HALF, HALF)
    k_here, v_here = k_in.at[here], v_in.at[here]

    def send_cached(i, _):
        to = lax.rem(seq + i, SEQ)
        there = head_at(section, to)
        push(keys.at[core, :, columns(there)], k_here, send.at[0], recv.at[0], (section, to))
        push(vals.at[core, :, columns(there)], v_here, send.at[1], recv.at[1], (section, to))
        return 0

    def query_rows(to_section, to):
        return acts.at[rows_of(group_at(to_section, to) * RB, RB), columns(head_at(to_section, to))]

    def send_query(to_section, to):
        push(query_rows(to_section, to), q_in.at[me], send.at[3], recv.at[3 + section], (to_section, to))

    def send_queries():
        for j in range(1, SECT):
            send_query(lax.rem(section + j, SECT), seq)

        def some(i, _):
            for j in range(SECT):
                send_query(lax.rem(section + j, SECT), lax.rem(seq + i, SEQ))
            return 0

        lax.fori_loop(1, SEQ, some, 0)

    def top_rows(to):
        return top.at[rows_of(group_at(section, to) * RB, RB), columns(head_at(section, to))]

    def send_top(i, _):
        to = lax.rem(seq + i, SEQ)
        push(top_rows(to), up_s.at[seq], send.at[2], recv.at[2], (section, to))
        return 0

    keep(keys.at[core, :, columns(head)], k_here, recv.at[0])
    keep(vals.at[core, :, columns(head)], v_here, recv.at[1])
    keep(top_rows(seq), up_s.at[seq], recv.at[2])
    keep(query_rows(section, seq), q_in.at[me], recv.at[3 + section])
    keep(gain.at[chip], g_in.at[section], recv.at[7])

    lax.fori_loop(1, SEQ, send_cached, 0)
    pl.semaphore_wait(ready, SECT - 1)
    @pl.when(section == SECT - 1)
    def _():
        send_queries()

    for j in range(1, SECT):
        to_section = lax.rem(section + j, SECT)
        push(gain.at[lax.div(to_section, 2)], g_in.at[section], send.at[4], recv.at[7], (to_section, seq))
    lax.fori_loop(1, SEQ, send_top, 0)
    k_half, v_half = k_in.at[rows_of(core * KHALF, KHALF)], v_in.at[rows_of(core * KHALF, KHALF)]
    k_other, v_other = k_in.at[rows_of((1 - core) * KHALF, KHALF)], v_in.at[rows_of((1 - core) * KHALF, KHALF)]
    arrived(k_half, recv.at[0])
    push(k_half, k_half, send.at[5], recv.at[8], (sibling, seq))

    arrived(k_other, recv.at[8])
    kt = k_in[...].T
    kk[:DH, :] = kt
    kk[DH:, :] = kt
    arrived(v_half, recv.at[1])
    push(v_half, v_half, send.at[6], recv.at[9], (sibling, seq))
    arrived(v_other, recv.at[9])
    vt[...] = v_in[...].T
    @pl.when(section != SECT - 1)
    def _():
        send_queries()

    arrived(g_in, recv.at[7])
    arrived(q_in.at[pl.ds((SECT - 1) * SEQ, SEQ)], recv.at[3 + SECT - 1])
    q2_s[...] = split_query(load_query(q_in, g_in, 0, turn))
    peak = jnp.max(scores(turn, 0, kk, q2_s, bias, sc), axis=1, keepdims=True)
    arrived(up_s, recv.at[2])

    def send_grads(step):
        layer, t = at_step(step, turn)
        first = layer * SEQ + t * GRP

        def send_one(inside):
            push(
                grad.at[first + inside], acts_out.at[mine, columns(head)],
                send.at[7], recv.at[10], (layer, t * GRP + inside),
            )

        for k in range(1, GRP):
            send_one(lax.rem(seq + k, GRP))
        inside = lax.rem(seq, GRP)
        own = (layer == section) & (t == lax.div(seq, GRP))

        @pl.when(own)
        def _():
            keep(grad.at[first + inside], acts_out.at[mine, columns(head)], recv.at[10])

        @pl.when(jnp.logical_not(own))
        def _():
            send_one(inside)

    def attend(step, peak):
        layer = SECT - 1 - lax.div(step, TILES)

        @pl.when((lax.rem(step, TILES) == TILES - 1) & (layer > 0))
        def _():
            arrived(q_in.at[pl.ds((layer - 1) * SEQ, SEQ)], recv.at[2 + layer])

        return one_step(step, turn, peak, q_in, g_in, k_in, grad, kk, vt, bias, sc, ex, dp, dkv, q2_s, up_s)

    def attend_send(step, peak):
        peak = attend(step, peak)
        send_grads(step)
        return peak

    lax.fori_loop(0, STEPS, attend_send, peak)

    near_half = pl.ds(pl.multiple_of(core * KHALF, DH), KHALF)
    far_half = pl.ds(pl.multiple_of((1 - core) * KHALF, DH), KHALF)
    for kv in range(2):
        outgoing[kv] = dkv[kv, :, far_half].astype(jnp.bfloat16).T
        for far, sem in ((1 - side, 11 + kv), (side, 21 + kv)):
            rows = rows_of(far * SIDE, SIDE)
            push(outgoing.at[kv, rows], from_core.at[kv, rows], send.at[8 + kv], recv.at[sem], (sibling, seq))

    def add_core(kv, rows):
        return part[kv, rows].astype(jnp.float32) + from_core[kv, rows].astype(jnp.float32)

    def piece(p):
        return lax.rem(y + p, 2) * PROWS

    for kv in range(2):
        part[kv] = dkv[kv, :, near_half].astype(jnp.bfloat16).T
        arrived(from_core.at[kv, rows_of((1 - side) * SIDE, SIDE)], recv.at[11 + kv])
        for p in range(2):
            rows = rows_of((1 - side) * SIDE + piece(p), PROWS)
            part[kv, rows] = add_core(kv, rows).astype(jnp.bfloat16)
            push(
                part.at[kv, rows], from_chip.at[kv, rows_of(piece(p), PROWS)],
                send.at[10], recv.at[13 + 2 * kv + p], (section, partner),
            )

    def send_totals(kv, p, target):
        def some(i, _):
            which = lax.rem(2 * (x + z) + section + i, PBLOCKS)
            block = block_at(lax.rem(y + p, 2), which, side)
            src = total.at[kv, rows_of(piece(p) + which * HALF, HALF)]

            @pl.when(block == seq)
            def _():
                keep(src, target, recv.at[17 + kv])

            @pl.when(block != seq)
            def _():
                push(src, target, send.at[11 + kv], recv.at[17 + kv], (section, block))

            push(src, target, send.at[11 + kv], recv.at[17 + kv], (across, block))
            return 0

        lax.fori_loop(0, PBLOCKS, some, 0)

    for kv, out in ((0, k_out), (1, v_out)):
        for p in range(2):
            done = rows_of(piece(p), PROWS)
            if p == 0:
                arrived(from_core.at[kv, rows_of(side * SIDE, SIDE)], recv.at[21 + kv])
            arrived(from_chip.at[kv, done], recv.at[13 + 2 * kv + p])
            total[kv, done] = (
                add_core(kv, rows_of(side * SIDE + piece(p), PROWS)) + from_chip[kv, done].astype(jnp.float32)
            ).astype(jnp.bfloat16)
            send_totals(kv, p, out.at[core, :, columns(head)])

    for kv, out in ((0, k_out), (1, v_out)):
        arrived(out.at[core], recv.at[17 + kv])
        push(out.at[core], out.at[core], send.at[13 + kv], recv.at[19 + kv], (sibling, seq))
    arrived(acts_out, recv.at[10])
    for kv, out in ((0, k_out), (1, v_out)):
        arrived(out.at[1 - core], recv.at[19 + kv])

    arrived(k_in.at[: (SEQ - 1) * HALF], send.at[0])
    arrived(v_in.at[: (SEQ - 1) * HALF], send.at[1])
    arrived(up_s.at[: SEQ - 1], send.at[2])
    arrived(q_in.at[: ALL - 1], send.at[3])
    arrived(g_in.at[: SECT - 1], send.at[4])
    arrived(k_half, send.at[5])
    arrived(v_half, send.at[6])
    arrived(grad.at[: ALL - 1], send.at[7])
    arrived(from_chip, send.at[10])
    for kv, out in ((0, k_out), (1, v_out)):
        arrived(outgoing.at[kv], send.at[8 + kv])
        arrived(k_in.at[: (SEQ - 1) * HALF], send.at[11 + kv])
        arrived(out.at[core], send.at[13 + kv])


def attention_grads(offs, acts, top, keys, vals, gains):
    bf = jnp.bfloat16
    any_space = pl.BlockSpec(memory_space=pl.ANY)
    return pl.pallas_call(
        fused_kernel,
        out_shape=(
            jax.ShapeDtypeStruct((SECT * RB, SEQ * DH), bf),
            jax.ShapeDtypeStruct((2, HALF, SEQ * DH), bf),
            jax.ShapeDtypeStruct((2, HALF, SEQ * DH), bf),
        ),
        in_specs=[pl.BlockSpec(memory_space=pltpu.SMEM)] + [any_space] * 4 + [pl.BlockSpec(memory_space=pltpu.VMEM)],
        out_specs=(any_space, any_space, any_space),
        scratch_shapes=[
            pltpu.VMEM((ALL, RB, DH), bf),
            pltpu.VMEM((SEQ, RB, DH), bf),
            pltpu.VMEM((KLEN, DH), bf),
            pltpu.VMEM((KLEN, DH), bf),
            pltpu.VMEM((SECT, 8, DH), jnp.float32),
            pltpu.VMEM((ALL, RB, DH), bf),
            pltpu.VMEM((2 * DH, KLEN), bf),
            pltpu.VMEM((DH, KLEN), bf),
            pltpu.VMEM((TILES, TILE, KLEN), jnp.float32),
            pltpu.VMEM((2, TILE, KLEN), jnp.float32),
            pltpu.VMEM((TILE, KLEN), bf),
            pltpu.VMEM((TILE, KLEN), jnp.float32),
            pltpu.VMEM((2, DH, KLEN), jnp.float32),
            pltpu.VMEM((TILE, 2 * DH), bf),
            pltpu.VMEM((2, KHALF, DH), bf),
            pltpu.VMEM((2, KHALF, DH), bf),
            pltpu.VMEM((2, KHALF, DH), bf),
            pltpu.VMEM((2, SIDE, DH), bf),
            pltpu.VMEM((2, SIDE, DH), bf),
            pltpu.VMEM((2, 8, DH), jnp.float32),
            pltpu.SemaphoreType.DMA((15,)),
            pltpu.SemaphoreType.DMA((23,)),
            pltpu.SemaphoreType.REGULAR,
        ],
        compiler_params=pltpu.CompilerParams(
            collective_id=0, has_side_effects=True, vmem_limit_bytes=60 * 2**20
        ),
    )(offs, acts, top, keys, vals, gains)


def store_kernel(a, b, c, a_out, b_out, c_out, a_tmp, b_tmp, c_tmp, sems):
    parts = []
    for src, tmp, dst in ((a, a_tmp, a_out), (b, b_tmp, b_out), (c, c_tmp, c_out)):
        half = src.shape[1] // 2
        for cols in (slice(0, half), slice(half, 2 * half)):
            n = len(parts)
            parts.append((
                pltpu.make_async_copy(src.at[:, cols], tmp.at[:, cols], sems.at[0, n]),
                pltpu.make_async_copy(tmp.at[:, cols], dst.at[:, cols], sems.at[1, n]),
            ))
    for load, _ in parts:
        load.start()
    for load, save in parts:
        load.wait()
        save.start()
    for _, save in parts:
        save.wait()


def store(*arrays):
    any_space = pl.BlockSpec(memory_space=pl.ANY)
    return pl.pallas_call(
        store_kernel,
        out_shape=tuple(jax.ShapeDtypeStruct(a.shape, a.dtype) for a in arrays),
        in_specs=[any_space] * 3,
        out_specs=(any_space,) * 3,
        scratch_shapes=[pltpu.VMEM(a.shape, a.dtype) for a in arrays] + [pltpu.SemaphoreType.DMA((2, 6))],
    )(*arrays)


def local(acts, gains, grad_top, keys, values, offsets):
    out_acts, out_keys, out_values = attention_grads(
        offsets, acts[0], grad_top, keys.reshape(2, HALF, -1), values.reshape(2, HALF, -1), gains
    )
    out_acts, out_keys, out_values = store(
        out_acts, out_keys.reshape(2 * HALF, -1), out_values.reshape(2 * HALF, -1)
    )
    return (out_acts[None], out_keys, out_values)


def solution(mesh):
    return jax.shard_map(
        local,
        mesh=mesh,
        in_specs=(
            P("section", "seq", None),
            P("section", None),
            P("seq", None),
            P("seq", None),
            P("seq", None),
            P(),
        ),
        out_specs=(P("section", "seq", None), P("seq", None), P("seq", None)),
        check_vma=False,
    )
```
